256 devices in a mesh: gx: 16 (over z, core), gy: 4 (over x), gz: 4 (over y).
Axes of the slice: x: 4, y: 4, z: 8, core: 2. Of those that a mesh axis runs over, the one named last changes fastest.
Arguments:
- a_blocks: bfloat16 [64, 16, 8, 7, 4096], P('gx', 'gy', 'gz'), may hold values from -6 to 6
- prolong: bfloat16 [64, 16, 8, 4096], P('gx', 'gy', 'gz'), may hold values from -0.75 to 0.75
- pairing: int32 [32, 8, 8], P('gx', 'gy', 'gz'), may hold values 0 or 1
- route: int32 [4096, 1], P(('gx', 'gy', 'gz')), may hold values from 0 to 15; in each aligned block of 16 rows (0 to 15, 16 to 31, ...) at most 2 rows name the same one
Outputs:
- coarse_rows: bfloat16 [8192, 11, 4096], P(('gx', 'gy', 'gz'))
The draws below stay inside these ranges and needn't reach their ends.
Inputs may be any that keep to these rules, and one draw needn't show every extreme that they name: `pairing`: 0 pairs each patch's elements along the first direction, 1 along the second. `route`: among the 16 aggregates of one device no destination is named more than 2 times, and in every draw some device names one destination exactly 2 times.
All inputs are finite; a program needn't handle non-finite values. No bound on the sum of `pairing` on one device may be relied on, other than what follows from the above.
Results may differ from the reference program's by a relative error of at most 0.0049.
Values may be sent and summed in bfloat16 or wider, within the bound.
A program may use at most 128 MiB of HBM per device.

```python
import math
import jax
import jax.numpy as jnp
import numpy as np
from jax import lax

BLK = 64
FACES = 7
COARSE = 11
CX = 4
CY = 4
CZ = 2
NX = 64
NY = 16
NZ = 8
AGG_DEV = 16
NAGG = 4096
CAP = 2
N_GX = 16
N_GY = 4
N_GZ = 4
DEVICES = 256


def touch_ends(values, own_key, smallest, high):
    shape = values.shape
    index_at = [jax.random.randint(jax.random.fold_in(own_key, axis), (), 0, shape[axis]) for axis in range(len(shape))]
    values = values.at[tuple(index_at)].set(smallest)
    longest = shape.index(max(shape))
    index_at[longest] = (index_at[longest] + 1) % shape[longest]
    return values.at[tuple(index_at)].set(high)


def level_of(own_key, dims, cuts, smallest, largest):
    factor_of, own = 1.0, jax.random.fold_in(own_key, 6)
    for axis_at, parts in cuts:
        heights = jnp.exp(jax.random.uniform(jax.random.fold_in(own, axis_at), (parts,), jnp.float32, smallest / len(cuts), largest / len(cuts)))
        factor_of = factor_of * jnp.repeat(heights, dims[axis_at] // parts).reshape([-1 if axis == axis_at else 1 for axis in range(len(dims))])
    return factor_of


def routed_block(stream_key, own, number, rows, count, top, reach, lean):
    order = jax.random.permutation(stream_key, count)
    packed, common = load_shares(count, rows * top, reach, lean, True), load_shares(count, rows * top, reach, lean, False)
    places = jnp.arange(count)

    def named(lengths, rotation):
        used = int((lengths > 0).sum())
        fixed = max(1, used // 4)
        moved = fixed + (places - fixed + rotation * (used - fixed)) % max(1, count - fixed)
        return jnp.zeros((count,), jnp.int32).at[order[jnp.where(places < fixed, places, moved)]].set(jnp.asarray(lengths, jnp.int32))

    lengths = jnp.where(number % 4 == 0, named(packed, number // 4), named(common, number - number // 4 - 1))
    mixed = jax.random.permutation(jax.random.fold_in(own, 3), count)
    giver, receiver = mixed[0:count // 2 * 2:2], mixed[1:count // 2 * 2:2]
    room = jnp.minimum(lengths[giver] - 1, reach - lengths[receiver]) // 2
    room = jnp.where((giver == order[0]) | (receiver == order[0]) | (lengths[receiver] == 0), 0, jnp.maximum(room, 0))
    moved = jax.random.randint(jax.random.fold_in(own, 4), (count // 2,), 0, 1 << 20) % (room + 1)
    lengths = lengths.at[giver].add(-moved).at[receiver].add(moved)
    labels = jnp.searchsorted(jnp.cumsum(lengths), jnp.arange(rows * top), side="right").astype(jnp.int32)
    listing = labels.reshape(top, rows).T
    listing = listing[jax.random.permutation(jax.random.fold_in(own, 1), rows)]
    rotation = jax.random.randint(jax.random.fold_in(own, 2), (rows, 1), 0, top)
    return jnp.take_along_axis(listing, (jnp.arange(top)[None, :] + rotation) % top, axis=1)


def load_shares(amount, total, most, skew, full):
    loads = [(1 << 20) // math.isqrt(rank ** skew) + 1 for rank in range(1, amount + 1)]
    largest = most if full else min(most, max(-(-total // amount), total * loads[0] // sum(loads)))
    least = 1 if total - largest >= amount - 1 else 0
    given, surplus = [largest] + [least] * (amount - 1), total - largest - least * (amount - 1)
    while surplus > 0:
        free = [i for i in range(1, amount) if given[i] < largest] or [i for i in range(1, amount) if given[i] < most]
        mass, left = sum([loads[i] for i in free]), surplus
        for i in free:
            extra = min(most - given[i], max(1, left * loads[i] // mass), surplus)
            given[i] = given[i] + extra
            surplus = surplus - extra
    return np.array(given)


def scatter_about(own_key, shape, width, reach, pieces=(), held_as=jnp.bfloat16):
    values = width * jax.random.normal(own_key, shape, jnp.float32)
    if pieces:
        values = values * level_of(own_key, shape, pieces, -0.22, 0.18)
    return jnp.clip(values, -reach, reach).astype(held_as)


def setup_inputs(seed: int = 0) -> dict:
    key_list = jax.random.split(jax.random.key(seed), 5)
    a_blocks = scatter_about(key_list[0], (NX, NY, NZ, FACES, BLK * BLK), 1.0, 6.0, ((0, 16), (1, 4), (2, 4)))
    prolong = scatter_about(key_list[1], (NX, NY, NZ, BLK * BLK), BLK ** -0.5, 0.75, ((0, 16), (1, 4), (2, 4)))
    pairing = touch_ends((jax.random.randint(key_list[2], (NX // 2, NY // 2, NZ), 0, 2) < 1).astype(jnp.int32), jax.random.fold_in(key_list[2], 1), 0, 1)
    route_keys = jax.random.split(jax.random.fold_in(key_list[3], 1), NAGG // AGG_DEV)
    route_turns = jax.random.permutation(jax.random.fold_in(key_list[3], 3), NAGG // AGG_DEV)
    route = jax.vmap(lambda own, number: routed_block(jax.random.fold_in(key_list[3], 2), own, number, AGG_DEV, N_GX, 1, CAP, 2))(route_keys, route_turns).reshape((NAGG, 1))
    return {"a_blocks": a_blocks, "prolong": prolong, "pairing": pairing, "route": route}


x_first_order = [0, 2, 1, 3, 4, 5, 6]
x_second_order = [0, 1, 2, 3, 4, 5, 6]
y_first_order = [0, 4, 1, 2, 3, 5, 6]
y_second_order = [0, 3, 1, 2, 4, 5, 6]


def neighbours(padded):
    shifted = [padded[1:-1, 1:-1, 1:-1], padded[:-2, 1:-1, 1:-1], padded[2:, 1:-1, 1:-1],
               padded[1:-1, :-2, 1:-1], padded[1:-1, 2:, 1:-1], padded[1:-1, 1:-1, :-2],
               padded[1:-1, 1:-1, 2:]]
    return jnp.stack(shifted, axis=3)


def triple(blocks, nearby):
    leading = blocks.shape[:-1]
    left_mat = blocks.reshape(leading + (BLK, BLK)).astype(jnp.float32)
    right_mat = nearby.reshape(leading + (BLK, BLK)).astype(jnp.float32)
    own_block = jnp.swapaxes(right_mat[..., :1, :, :], -1, -2)
    product = jnp.matmul(left_mat, right_mat, precision=lax.Precision.HIGHEST)
    product = lax.optimization_barrier(product.astype(jnp.bfloat16)).astype(jnp.float32)
    result = jnp.matmul(own_block, product, precision=lax.Precision.HIGHEST)
    return result.reshape(leading + (BLK * BLK,))


def members(element_grid, pairs):
    size_x, size_y, size_z = element_grid.shape[:3]
    trailing = element_grid.shape[3:]
    patches = element_grid.reshape((size_x // 2, 2, size_y // 2, 2, size_z) + trailing)

    def pick(upper, lower, slot_order):
        return jnp.take(patches[:, upper, :, lower], jnp.array(slot_order, dtype=jnp.int32), axis=3)

    x_one = jnp.stack([pick(0, 0, x_first_order), pick(0, 1, x_first_order)], axis=3)
    x_two = jnp.stack([pick(1, 0, x_second_order), pick(1, 1, x_second_order)], axis=3)
    y_one = jnp.stack([pick(0, 0, y_first_order), pick(1, 0, y_first_order)], axis=3)
    y_two = jnp.stack([pick(0, 1, y_second_order), pick(1, 1, y_second_order)], axis=3)
    along_x = (pairs == 0).reshape(pairs.shape + (1,) * (x_one.ndim - 3))
    member_one = jnp.where(along_x, x_one, y_one)
    member_two = jnp.where(along_x, x_two, y_two)
    return member_one.reshape((-1,) + member_one.shape[4:]), member_two.reshape((-1,) + member_two.shape[4:])


def arrange(member_one, member_two):
    diagonal = member_one[..., 0, :] + member_two[..., 0, :] + member_one[..., 1, :] + member_two[..., 1, :]
    return jnp.concatenate([diagonal[..., None, :], member_one[..., 2:, :], member_two[..., 2:, :]], axis=-2)


def slot_sources(routes, n_dest, capacity):
    total = routes.shape[0]
    chosen = (routes[:, None] == jnp.arange(n_dest, dtype=jnp.int32)[None, :]).astype(jnp.int32)
    before = (jnp.cumsum(chosen, axis=0) - chosen).astype(jnp.int32)
    ranking = jnp.sum(before * chosen, axis=1).astype(jnp.int32)
    position = routes * capacity + ranking
    targets = jnp.arange(n_dest * capacity, dtype=jnp.int32)
    matches = position[None, :] == targets[:, None]
    anchor = jnp.sum(jnp.where(matches, jnp.arange(total, dtype=jnp.int32)[None, :], 0), axis=1).astype(jnp.int32)
    filled = jnp.any(matches, axis=1)
    return anchor, filled


def pack_slots(payload, anchor, filled):
    taken = jnp.take(payload, anchor, axis=0)
    keep_row = filled.reshape(filled.shape + (1,) * (payload.ndim - 1))
    return jnp.where(keep_row, taken, jnp.zeros_like(taken))


def reference(a_blocks, prolong, pairing, route):
    padded = jnp.pad(prolong, ((1, 1), (1, 1), (1, 1), (0, 0)))
    routes_all = route[:, 0].reshape(N_GX, N_GY * N_GZ, AGG_DEV)

    def one_slab(inputs):
        slab_index, slab_dest = inputs
        first_row = (slab_index * CX).astype(jnp.int32)
        blocks = lax.dynamic_slice_in_dim(a_blocks, first_row, CX, 0)
        beside_all = lax.dynamic_slice_in_dim(padded, first_row, CX + 2, 0)
        slab_pairs = lax.dynamic_slice_in_dim(pairing, (slab_index * (CX // 2)).astype(jnp.int32), CX // 2, 0)
        galerkin = triple(blocks, neighbours(beside_all))
        member_one, member_two = members(galerkin, slab_pairs)
        coarse = arrange(member_one, member_two).astype(jnp.bfloat16)
        coarse = coarse.reshape(CX // 2, N_GY, CY // 2, N_GZ, CZ, 2, COARSE, BLK * BLK)
        coarse = coarse.transpose(1, 3, 0, 2, 4, 5, 6, 7).reshape(N_GY * N_GZ, AGG_DEV, COARSE, BLK * BLK)

        def send_one(device_rows, device_dest):
            anchor, filled = slot_sources(device_dest, N_GX, CAP)
            return pack_slots(device_rows, anchor, filled)

        return jax.vmap(send_one)(coarse, slab_dest)

    buffers = lax.map(one_slab, (jnp.arange(N_GX, dtype=jnp.int32), routes_all))
    buffers = buffers.reshape(N_GX, N_GY * N_GZ, N_GX, CAP, COARSE, BLK * BLK)
    return buffers.transpose(2, 1, 0, 3, 4, 5).reshape(DEVICES * N_GX * CAP, COARSE, BLK * BLK)
```

```python
import math

import jax
import jax.numpy as jnp
from jax import lax
from jax.sharding import PartitionSpec as P

x_first_order = [0, 2, 1, 3, 4, 5, 6]
x_second_order = [0, 1, 2, 3, 4, 5, 6]
y_first_order = [0, 4, 1, 2, 3, 5, 6]
y_second_order = [0, 3, 1, 2, 4, 5, 6]


def padded_2(array, sides, width):
    for axis, dim in sides:
        devices, length = (lax.axis_size(axis), array.shape[dim])
        up = [(i, (i + 1) % devices) for i in range(devices - 1)]
        down = [(j, i) for i, j in up]
        last = lax.slice_in_dim(array, length - width, length, axis=dim)
        initial = lax.slice_in_dim(array, 0, width, axis=dim)
        before = lax.ppermute(last, axis, up)
        after = lax.ppermute(initial, axis, down)
        array = jnp.concatenate([before, array, after], axis=dim)
    return array


def neighbours(padded):
    shifted = [
        padded[1:-1, 1:-1, 1:-1],
        padded[:-2, 1:-1, 1:-1],
        padded[2:, 1:-1, 1:-1],
        padded[1:-1, :-2, 1:-1],
        padded[1:-1, 2:, 1:-1],
        padded[1:-1, 1:-1, :-2],
        padded[1:-1, 1:-1, 2:],
    ]
    return jnp.stack(shifted, axis=3)


def triple(blocks, nearby):
    block_side = math.isqrt(blocks.shape[-1])
    leading = blocks.shape[:-1]
    left_mat = blocks.reshape(leading + (block_side, block_side))
    right_mat = nearby.reshape(leading + (block_side, block_side))
    own_block = jnp.swapaxes(right_mat[..., :1, :, :], -1, -2)
    product = jnp.matmul(left_mat, right_mat, preferred_element_type=jnp.float32).astype(
        jnp.bfloat16
    )
    result = jnp.matmul(own_block, product, preferred_element_type=jnp.float32)
    return result.reshape(leading + (block_side * block_side,))


def members(element_grid, pairs):
    size_x, size_y, size_z = element_grid.shape[:3]
    trailing = element_grid.shape[3:]
    patches = element_grid.reshape((size_x // 2, 2, size_y // 2, 2, size_z) + trailing)

    def pick(upper, lower, slot_order):
        return jnp.take(patches[:, upper, :, lower], jnp.array(slot_order, dtype=jnp.int32), axis=3)

    x_one = jnp.stack([pick(0, 0, x_first_order), pick(0, 1, x_first_order)], axis=3)
    x_two = jnp.stack([pick(1, 0, x_second_order), pick(1, 1, x_second_order)], axis=3)
    y_one = jnp.stack([pick(0, 0, y_first_order), pick(1, 0, y_first_order)], axis=3)
    y_two = jnp.stack([pick(0, 1, y_second_order), pick(1, 1, y_second_order)], axis=3)
    along_x = (pairs == 0).reshape(pairs.shape + (1,) * (x_one.ndim - 3))
    member_one = jnp.where(along_x, x_one, y_one)
    member_two = jnp.where(along_x, x_two, y_two)
    return (
        member_one.reshape((-1,) + member_one.shape[4:]),
        member_two.reshape((-1,) + member_two.shape[4:]),
    )


def arrange(member_one, member_two):
    diagonal = (
        member_one[..., 0, :]
        + member_two[..., 0, :]
        + member_one[..., 1, :]
        + member_two[..., 1, :]
    )
    return jnp.concatenate(
        [diagonal[..., None, :], member_one[..., 2:, :], member_two[..., 2:, :]], axis=-2
    )


def slot_sources(routes, n_dest, capacity):
    total = routes.shape[0]
    chosen = (routes[:, None] == jnp.arange(n_dest, dtype=jnp.int32)[None, :]).astype(jnp.int32)
    before = jnp.cumsum(chosen, axis=0) - chosen
    ranking = jnp.sum(before * chosen, axis=1)
    position = routes * capacity + ranking
    targets = jnp.arange(n_dest * capacity, dtype=jnp.int32)
    matches = position[None, :] == targets[:, None]
    anchor = jnp.sum(jnp.where(matches, jnp.arange(total, dtype=jnp.int32)[None, :], 0), axis=1)
    filled = jnp.any(matches, axis=1)
    return (anchor, filled)


def pack_slots(payload, anchor, filled):
    taken = jnp.take(payload, anchor, axis=0)
    keep_row = filled.reshape(filled.shape + (1,) * (payload.ndim - 1))
    return jnp.where(keep_row, taken, jnp.zeros_like(taken))


def local(a_blocks, prolong, pairing, route):
    padded = padded_2(prolong, (("gx", 0), ("gy", 1), ("gz", 2)), 1)
    nearby = neighbours(padded)
    devices_gx = lax.axis_size("gx")
    aggregates = route.shape[0]
    capacity = max(2, 3 * aggregates // (2 * devices_gx))
    anchor, filled = slot_sources(route[:, 0], devices_gx, capacity)
    galerkin = triple(a_blocks, nearby)
    member_one, member_two = members(galerkin, pairing)
    coarse = arrange(member_one, member_two).astype(jnp.bfloat16)
    return lax.all_to_all(
        pack_slots(coarse, anchor, filled), "gx", split_axis=0, concat_axis=0, tiled=True
    )


def solution(mesh):
    placed = (
        P("gx", "gy", "gz", None, None),
        P("gx", "gy", "gz", None),
        P("gx", "gy", "gz"),
        P(("gx", "gy", "gz"), None),
    )
    return jax.shard_map(
        local,
        mesh=mesh,
        in_specs=placed,
        out_specs=P(("gx", "gy", "gz"), None, None),
        check_vma=False,
    )
```

```python
import jax
import jax.numpy as jnp
from jax import lax
from jax.experimental import pallas as pl
from jax.experimental.pallas import tpu as pltpu
from jax.sharding import PartitionSpec as P

MESH = pl.DeviceIdType.MESH
F32 = jnp.float32
BF16 = jnp.bfloat16
GX, GY, GZ = 16, 4, 4


def iota(shape, dim):
    return lax.broadcasted_iota(jnp.int32, shape, dim)


def ones_where(cond):
    return jnp.where(cond, 1.0, 0.0).astype(BF16)


def dot(a, b):
    return jnp.dot(a, b, preferred_element_type=F32)


def kernel(pair_ref, route_ref, a_ref, p_ref, out_ref,
           nn, nr, ppt, hx, hy, hz, zs, gal, rows, send, recv, anchors,
           hs_sem, hr_sem, s_sem, r_sem):
    gx, gy, gz = lax.axis_index("gx"), lax.axis_index("gy"), lax.axis_index("gz")

    barrier = pltpu.get_barrier_semaphore()

    def greet(k, carry):
        pl.semaphore_signal(barrier, inc=1, device_id={"gx": lax.rem(gx + k, GX)}, device_id_type=MESH)
        return carry

    lax.fori_loop(1, GX, greet, 0)
    sides = (
        (gx > 0, {"gx": gx - 1}), (gx < GX - 1, {"gx": gx + 1}),
        (gy > 0, {"gy": gy - 1}), (gy < GY - 1, {"gy": gy + 1}),
        (gz > 0, {"gz": gz - 1}), (gz < GZ - 1, {"gz": gz + 1}),
    )
    for there, device in sides[2:]:
        @pl.when(there)
        def _():
            pl.semaphore_signal(barrier, inc=1, device_id=device, device_id_type=MESH)

    left = iota((64, 128), 1) < 64

    ci, ki = iota((64, 128), 0), iota((64, 128), 1)
    order = ones_where(((ki // 2) % 32 == ci // 2) & (ki // 64 == (ci + ki) % 2))
    ri, li = iota((128, 128), 0), iota((128, 128), 1)
    spread = ones_where(li % 64 == 2 * (ri % 32) + (ri // 32) % 2)
    same_z = li % 2 == ri // 64
    z_lane = (ri % 2) == (li // 64)
    half_row = (ri // 64) == (li // 64)

    def prepare(i, carry):
        for u in range(2):
            xy = 2 * i + u
            raw = p_ref[xy].astype(F32)
            both = jnp.concatenate([raw, pltpu.roll(raw, 64, 1)], axis=0)
            tile = dot(order, jnp.where(z_lane, both, 0.0).astype(BF16))
            nn[xy // 4, xy % 4] = tile.astype(BF16)
            turned = pltpu.roll(tile, 64, 1)
            nr[xy] = turned.astype(BF16)
            twice = jnp.concatenate([raw, raw], axis=0)
            twice = jnp.where(half_row, twice, 0.0).astype(BF16)
            t = lax.dot_general(spread, twice, (((1,), (1,)), ((), ())), preferred_element_type=F32)
            ppt[xy] = jnp.where(same_z, t, 0.0).astype(BF16)
            if u == 0:
                low, high = tile, turned
            else:
                zs[0, i] = jnp.where(left, low, turned).astype(BF16)
                zs[1, i] = jnp.where(left, high, tile).astype(BF16)
        return carry

    lax.fori_loop(0, 8, prepare, 0)

    near = jnp.int32(GX - 1)
    for there, _ in sides[2:]:
        near = near + there.astype(jnp.int32)
    pl.semaphore_wait(barrier, near)

    faces = (
        (nn.at[0], hx.at[1]), (nn.at[3], hx.at[0]),
        (nn.at[:, 0], hy.at[1]), (nn.at[:, 3], hy.at[0]),
        (zs.at[0], hz.at[1]), (zs.at[1], hz.at[0]),
    )
    own_halo = (hx.at[0], hx.at[1], hy.at[0], hy.at[1], hz.at[0], hz.at[1])

    def halo(i):
        source, target = faces[i]
        return pltpu.make_async_remote_copy(
            src_ref=source, dst_ref=target, send_sem=hs_sem.at[i], recv_sem=hr_sem.at[i],
            device_id=sides[i][1], device_id_type=MESH,
        )

    for i in range(6):
        @pl.when(sides[i][0])
        def _():
            halo(i).start()

        @pl.when(jnp.logical_not(sides[i][0]))
        def _():
            own_halo[i][...] = jnp.zeros(own_halo[i].shape, BF16)

    zero = jnp.zeros((64, 128), BF16)
    left32 = iota((32, 128), 1) < 64

    def product(xy, s, near_tile):
        wide = jnp.concatenate(
            [jnp.concatenate([near_tile, zero], axis=1), jnp.concatenate([zero, near_tile], axis=1)], axis=0
        )
        mixed = dot(a_ref[xy, s], wide).astype(BF16)
        mixed = jnp.concatenate([mixed[:, :128], mixed[:, 128:]], axis=0)
        g = dot(ppt[xy], mixed)
        gal[xy * 14 + 2 * s] = jnp.where(left32, g[0:32], pltpu.roll(g[32:64], 64, 1))
        gal[xy * 14 + 2 * s + 1] = jnp.where(left32, pltpu.roll(g[64:96], 64, 1), g[96:128])

    def loop(n, body):
        def step(i, carry):
            body(i)
            return carry
        lax.fori_loop(0, n, step, 0)

    @pl.loop(0, 4)
    def _(x):
        for y in range(4):
            product(x * 4 + y, 0, nn[x, y])

    @pl.loop(0, 3)
    def _(i):
        for k in range(4):
            product(i * 4 + 4 + k, 1, nn[i, k])
            product(i * 4 + k, 2, nn[i + 1, k])

    @pl.loop(0, 3)
    def _(i):
        for k in range(4):
            product(k * 4 + i + 1, 3, nn[k, i])
            product(k * 4 + i, 4, nn[k, i + 1])

    for i in range(6):
        @pl.when(sides[i][0])
        def _():
            j = i ^ 1
            source, target = faces[j]
            pltpu.make_async_remote_copy(
                src_ref=source, dst_ref=target, send_sem=hs_sem.at[j], recv_sem=hr_sem.at[j],
                device_id=sides[i][1], device_id_type=MESH,
            ).wait_recv()

    @pl.loop(0, 4)
    def _(k):
        product(k, 1, hx[0, k])
        product(12 + k, 2, hx[1, k])
        product(k * 4, 3, hy[0, k])
        product(k * 4 + 3, 4, hy[1, k])

    @pl.loop(0, 8)
    def _(q):
        below, above = hz[0, q].astype(F32), hz[1, q].astype(F32)
        below = (below, pltpu.roll(below, 64, 1))
        above = (pltpu.roll(above, 64, 1), above)
        for u in range(2):
            xy = 2 * q + u
            own = nr[xy]
            product(xy, 5, jnp.where(left, below[u].astype(BF16), own))
            product(xy, 6, jnp.where(left, own, above[u].astype(BF16)))

    @pl.loop(0, GX)
    def _(d):
        def look(k, state):
            one, two = state
            hit = route_ref[k] == d
            two = jnp.where(hit & (one < 16) & (two == 16), k, two)
            one = jnp.where(hit & (one == 16), k, one)
            return one, two

        one, two = lax.fori_loop(0, 16, look, (jnp.int32(16), jnp.int32(16)))
        anchors[2 * d] = one
        anchors[2 * d + 1] = two

    @pl.loop(0, 16)
    def _(k):
        a, b, z, t = k // 8, (k // 4) % 2, (k // 2) % 2, k % 2
        along = pair_ref[k // 2] == 0
        corner = a * 8 + b * 2
        first = jnp.where(along, corner + t, corner + 4 * t)
        second = jnp.where(along, corner + 4 + t, corner + 4 * t + 1)

        def block(xy, s):
            return gal[xy * 14 + 2 * s + z]

        rows[k, 0] = (
            block(first, 0) + block(second, 0)
            + block(first, jnp.where(along, 2, 4)) + block(second, jnp.where(along, 1, 3))
        ).astype(BF16)
        slots_x = ((1, 3, 4, 5, 6), (2, 3, 4, 5, 6))
        slots_y = ((1, 2, 3, 5, 6), (1, 2, 4, 5, 6))
        for i, xy in enumerate((first, second)):
            for j in range(5):
                rows[k, 1 + 5 * i + j] = block(xy, jnp.where(along, slots_x[i][j], slots_y[i][j])).astype(BF16)

    def pick(d, c):
        k = anchors[2 * d + c]
        row = rows[jnp.minimum(k, 15)]
        return jnp.where(k < 16, row, jnp.zeros_like(row))

    def outgoing(k):
        return pltpu.make_async_remote_copy(
            src_ref=send.at[k], dst_ref=recv.at[gx], send_sem=s_sem.at[k], recv_sem=r_sem.at[k],
            device_id={"gx": lax.rem(gx + k, GX)}, device_id_type=MESH,
        )

    @pl.loop(1, GX)
    def _(k):
        d = lax.rem(gx + k, GX)
        for c in range(2):
            send[k, c] = pick(d, c)
        outgoing(k).start()

    for c in range(2):
        recv[gx, c] = pick(gx, c)

    for i in range(6):
        @pl.when(sides[i][0])
        def _():
            halo(i).wait_send()

    pi, qi = iota((256, 256), 0), iota((256, 256), 1)
    turn = ones_where((qi % 32 == pi // 8) & (qi // 32 == pi % 8))

    for g in range(2):
        @pl.loop(8 * g, 8 * g + 8)
        def _(s):
            k = lax.rem(gx - s + GX, GX)

            @pl.when(k != 0)
            def _():
                pltpu.make_async_remote_copy(
                    src_ref=send.at[k], dst_ref=recv.at[s], send_sem=s_sem.at[k], recv_sem=r_sem.at[k],
                    device_id={"gx": s}, device_id_type=MESH,
                ).wait_recv()

        @pl.loop(0, 11)
        def _(b):
            parts = []
            for h in range(2):
                x = jnp.concatenate(
                    [recv[8 * g + 4 * h + s, c, b] for s in range(4) for c in range(2)], axis=0
                )
                parts.append(dot(turn, x).reshape(32, 8, 128))
            tile = jnp.concatenate(parts, axis=1).astype(BF16)
            for j in range(32):
                out_ref[b, pl.ds(16 * g, 16), pl.ds(128 * j, 128)] = tile[j]

    @pl.loop(1, GX)
    def _(k):
        outgoing(k).wait_send()


def local(a_blocks, prolong, pairing, route):
    a = a_blocks.reshape(4, 4, 2, 7, 32, 128).transpose(0, 1, 3, 4, 2, 5).reshape(16, 7, 64, 128)
    p = prolong.reshape(4, 4, 2, 32, 128).transpose(0, 1, 3, 2, 4).reshape(16, 64, 128)
    smem = pl.BlockSpec(memory_space=pltpu.SMEM)
    vmem = pl.BlockSpec(memory_space=pltpu.VMEM)
    out = pl.pallas_call(
        kernel,
        out_shape=jax.ShapeDtypeStruct((11, 32, 4096), BF16),
        in_specs=[smem, smem, vmem, vmem],
        out_specs=vmem,
        scratch_shapes=[
            pltpu.VMEM((4, 4, 64, 128), BF16),
            pltpu.VMEM((16, 64, 128), BF16),
            pltpu.VMEM((16, 128, 128), BF16),
            pltpu.VMEM((2, 4, 64, 128), BF16),
            pltpu.VMEM((2, 4, 64, 128), BF16),
            pltpu.VMEM((2, 8, 64, 128), BF16),
            pltpu.VMEM((2, 8, 64, 128), BF16),
            pltpu.VMEM((224, 32, 128), F32),
            pltpu.VMEM((16, 11, 32, 128), BF16),
            pltpu.VMEM((16, 2, 11, 32, 128), BF16),
            pltpu.VMEM((16, 2, 11, 32, 128), BF16),
            pltpu.SMEM((32,), jnp.int32),
            pltpu.SemaphoreType.DMA((6,)),
            pltpu.SemaphoreType.DMA((6,)),
            pltpu.SemaphoreType.DMA((16,)),
            pltpu.SemaphoreType.DMA((16,)),
        ],
        compiler_params=pltpu.CompilerParams(
            collective_id=0, has_side_effects=True, vmem_limit_bytes=48 << 20
        ),
        cost_estimate=pl.CostEstimate(flops=1 << 30, bytes_accessed=8 << 20, transcendentals=0),
    )(pairing.reshape(8), route.reshape(16), a, p)
    return out.transpose(1, 0, 2)


def solution(mesh):
    placed = (
        P("gx", "gy", "gz", None, None),
        P("gx", "gy", "gz", None),
        P("gx", "gy", "gz"),
        P(("gx", "gy", "gz"), None),
    )
    return jax.shard_map(
        local,
        mesh=mesh,
        in_specs=placed,
        out_specs=P(("gx", "gy", "gz"), None, None),
        check_vma=False,
    )
```

```python
import functools

import jax
import jax.numpy as jnp
from jax import lax
from jax.experimental import pallas as pl
from jax.experimental.pallas import tpu as pltpu
from jax.sharding import PartitionSpec as P

MESH = pl.DeviceIdType.MESH
F32 = jnp.float32
BF16 = jnp.bfloat16
GX, GY, GZ = 16, 4, 4
AXES = (
    ("gx", GX, lambda: lax.axis_index("gx")),
    ("gy", GY, lambda: lax.axis_index("gy")),
    ("gz", GZ, lambda: lax.axis_index("gz")),
)
GROUPS = GX // 2
CASES = (
    [()]
    + [(g, g + GROUPS) for g in range(GROUPS)]
    + [(g, g + GROUPS, h, h + GROUPS) for g in range(GROUPS) for h in range(g + 1, GROUPS)]
    + [tuple(range(GX))]
)


def iota(shape, dim):
    return lax.broadcasted_iota(jnp.int32, shape, dim)


def ones_where(cond):
    return jnp.where(cond, 1.0, 0.0).astype(BF16)


def dot(a, b):
    return jnp.dot(a, b, preferred_element_type=F32)


def kernel(pair_ref, route_ref, a_hbm, p_hbm, recv, rows, anchors, choice,
           a_ref, p_ref, nn, nr, ppt, hx, hy, hz, zs, gal, send, mine, seen_x, seen_y, seen_z,
           in_sem, hs_sem, hr_sem, s_sem, r_sem, fs_sem, fr_sem):
    gx, gy, gz = lax.axis_index("gx"), lax.axis_index("gy"), lax.axis_index("gz")

    load_p = pltpu.make_async_copy(p_hbm, p_ref, in_sem.at[0])
    load_a = pltpu.make_async_copy(a_hbm, a_ref, in_sem.at[1])
    load_p.start()
    load_a.start()
    barrier = pltpu.get_barrier_semaphore()
    for name, size, at in AXES:
        @pl.loop(1, size)
        def _(k):
            pl.semaphore_signal(barrier, inc=1, device_id={name: lax.rem(at() + k, size)}, device_id_type=MESH)
    sides = (
        (gx > 0, {"gx": gx - 1}), (gx < GX - 1, {"gx": gx + 1}),
        (gy > 0, {"gy": gy - 1}), (gy < GY - 1, {"gy": gy + 1}),
        (gz > 0, {"gz": gz - 1}), (gz < GZ - 1, {"gz": gz + 1}),
    )
    left = iota((64, 128), 1) < 64

    ci, ki = iota((64, 128), 0), iota((64, 128), 1)
    order = ones_where(((ki // 2) % 32 == ci // 2) & (ki // 64 == (ci + ki) % 2))
    ri, li = iota((128, 128), 0), iota((128, 128), 1)
    spread = ones_where(li % 64 == 2 * (ri % 32) + (ri // 32) % 2)
    same_z = li % 2 == ri // 64
    z_lane = (ri % 2) == (li // 64)
    half_row = (ri // 64) == (li // 64)

    def prepare(i, carry):
        for u in range(2):
            xy = 2 * i + u
            raw = p_ref[xy].astype(F32)
            both = jnp.concatenate([raw, pltpu.roll(raw, 64, 1)], axis=0)
            tile = dot(order, jnp.where(z_lane, both, 0.0).astype(BF16))
            nn[xy // 4, xy % 4] = tile.astype(BF16)
            turned = pltpu.roll(tile, 64, 1)
            nr[xy] = turned.astype(BF16)
            twice = jnp.concatenate([raw, raw], axis=0)
            twice = jnp.where(half_row, twice, 0.0).astype(BF16)
            t = lax.dot_general(spread, twice, (((1,), (1,)), ((), ())), preferred_element_type=F32)
            ppt[xy] = jnp.where(same_z, t, 0.0).astype(BF16)
            if u == 0:
                low, high = tile, turned
            else:
                zs[0, i] = jnp.where(left, low, turned).astype(BF16)
                zs[1, i] = jnp.where(left, high, tile).astype(BF16)
        return carry

    load_p.wait()
    lax.fori_loop(0, 8, prepare, 0)

    lane = iota((8, 128), 1)

    def anchor(d, flags):
        def look(k, state):
            one, two = state
            hit = route_ref[k, 0] == d
            two = jnp.where(hit & (one < 16) & (two == 16), k, two)
            one = jnp.where(hit & (one == 16), k, one)
            return one, two

        one, two = lax.fori_loop(0, 16, look, (jnp.int32(16), jnp.int32(16)))
        anchors[2 * d] = one
        anchors[2 * d + 1] = two
        return jnp.where((lane == d) & (two < 16), 1.0, flags)

    mine[0] = lax.fori_loop(0, GX, anchor, jnp.zeros((8, 128), F32))
    pl.semaphore_wait(barrier, GX + GY + GZ - 3)

    def tell(stage, k, seen):
        name, size, at = AXES[stage]
        return pltpu.make_async_remote_copy(
            src_ref=mine.at[stage], dst_ref=seen.at[k], send_sem=fs_sem.at[stage, k], recv_sem=fr_sem.at[stage, k],
            device_id={name: lax.rem(at() + k, size)}, device_id_type=MESH,
        )

    stages = (seen_x, seen_y, seen_z)

    def tell_all(stage):
        for k in range(1, AXES[stage][1]):
            tell(stage, k, stages[stage]).start()

    def hear_all(stage):
        flags = mine[stage]
        for k in range(1, AXES[stage][1]):
            tell(stage, k, stages[stage]).wait()
            flags = jnp.maximum(flags, stages[stage][k])
        return flags

    faces = (
        (nn.at[0], hx.at[1]), (nn.at[3], hx.at[0]),
        (nn.at[:, 0], hy.at[1]), (nn.at[:, 3], hy.at[0]),
        (zs.at[0], hz.at[1]), (zs.at[1], hz.at[0]),
    )
    own_halo = (hx.at[0], hx.at[1], hy.at[0], hy.at[1], hz.at[0], hz.at[1])

    def halo(i):
        source, target = faces[i]
        return pltpu.make_async_remote_copy(
            src_ref=source, dst_ref=target, send_sem=hs_sem.at[i], recv_sem=hr_sem.at[i],
            device_id=sides[i][1], device_id_type=MESH,
        )

    for i in range(6):
        @pl.when(sides[i][0])
        def _():
            halo(i).start()

        @pl.when(jnp.logical_not(sides[i][0]))
        def _():
            own_halo[i][...] = jnp.zeros(own_halo[i].shape, BF16)

    tell_all(0)
    load_a.wait()
    zero = jnp.zeros((64, 128), BF16)
    left32 = iota((32, 128), 1) < 64

    def product(xy, s, near_tile):
        wide = jnp.concatenate(
            [jnp.concatenate([near_tile, zero], axis=1), jnp.concatenate([zero, near_tile], axis=1)], axis=0
        )
        mixed = dot(a_ref[xy, s], wide).astype(BF16)
        mixed = jnp.concatenate([mixed[:, :128], mixed[:, 128:]], axis=0)
        g = dot(ppt[xy], mixed)
        gal[xy * 14 + 2 * s] = jnp.where(left32, g[0:32], pltpu.roll(g[32:64], 64, 1))
        gal[xy * 14 + 2 * s + 1] = jnp.where(left32, pltpu.roll(g[64:96], 64, 1), g[96:128])

    def loop(n, body):
        def step(i, carry):
            body(i)
            return carry
        lax.fori_loop(0, n, step, 0)

    @pl.loop(0, 4)
    def _(x):
        for y in range(4):
            product(x * 4 + y, 0, nn[x, y])

    @pl.loop(0, 3)
    def _(i):
        for k in range(4):
            product(i * 4 + 4 + k, 1, nn[i, k])
            product(i * 4 + k, 2, nn[i + 1, k])

    @pl.loop(0, 3)
    def _(i):
        for k in range(4):
            product(k * 4 + i + 1, 3, nn[k, i])
            product(k * 4 + i, 4, nn[k, i + 1])

    mine[1] = hear_all(0)
    tell_all(1)

    for i in range(6):
        @pl.when(sides[i][0])
        def _():
            j = i ^ 1
            source, target = faces[j]
            pltpu.make_async_remote_copy(
                src_ref=source, dst_ref=target, send_sem=hs_sem.at[j], recv_sem=hr_sem.at[j],
                device_id=sides[i][1], device_id_type=MESH,
            ).wait_recv()

    @pl.loop(0, 4)
    def _(k):
        product(k, 1, hx[0, k])
        product(12 + k, 2, hx[1, k])
        product(k * 4, 3, hy[0, k])
        product(k * 4 + 3, 4, hy[1, k])

    @pl.loop(0, 8)
    def _(q):
        below, above = hz[0, q].astype(F32), hz[1, q].astype(F32)
        below = (below, pltpu.roll(below, 64, 1))
        above = (pltpu.roll(above, 64, 1), above)
        for u in range(2):
            xy = 2 * q + u
            own = nr[xy]
            product(xy, 5, jnp.where(left, below[u].astype(BF16), own))
            product(xy, 6, jnp.where(left, own, above[u].astype(BF16)))

    mine[2] = hear_all(1)
    tell_all(2)

    @pl.loop(0, 16)
    def _(k):
        a, b, z, t = k // 8, (k // 4) % 2, (k // 2) % 2, k % 2
        along = pair_ref[a, b, z] == 0
        corner = a * 8 + b * 2
        first = jnp.where(along, corner + t, corner + 4 * t)
        second = jnp.where(along, corner + 4 + t, corner + 4 * t + 1)

        def block(xy, s):
            return gal[xy * 14 + 2 * s + z]

        rows[k, 0] = (
            block(first, 0) + block(second, 0)
            + block(first, jnp.where(along, 2, 4)) + block(second, jnp.where(along, 1, 3))
        ).astype(BF16)
        slots_x = ((1, 3, 4, 5, 6), (2, 3, 4, 5, 6))
        slots_y = ((1, 2, 3, 5, 6), (1, 2, 4, 5, 6))
        for i, xy in enumerate((first, second)):
            for j in range(5):
                rows[k, 1 + 5 * i + j] = block(xy, jnp.where(along, slots_x[i][j], slots_y[i][j])).astype(BF16)

    def outgoing(k):
        return pltpu.make_async_remote_copy(
            src_ref=send.at[k], dst_ref=recv.at[gx], send_sem=s_sem.at[k], recv_sem=r_sem.at[k],
            device_id={"gx": lax.rem(gx + k, GX)}, device_id_type=MESH,
        )

    @pl.loop(1, GX)
    def _(k):
        send[k] = pick(rows, anchors, lax.rem(gx + k, GX), 0)
        outgoing(k).start()

    recv[gx] = pick(rows, anchors, gx, 0)

    flags = hear_all(2)[0:1]
    flags = jnp.where(iota((1, 128), 1) < GROUPS, jnp.maximum(flags, pltpu.roll(flags, 128 - GROUPS, 1)), 0.0)
    place = iota((1, 128), 1).astype(F32)
    count = jnp.sum(flags)
    high = jnp.max(jnp.where(flags > 0, place, 0.0))
    low = jnp.min(jnp.where(flags > 0, place, 128.0))
    two = 1.0 + GROUPS + low * (2 * GROUPS - 1 - low) * 0.5 + (high - low - 1.0)
    case = jnp.where(count > 2.5, 1.0 * (len(CASES) - 1), jnp.where(count > 1.5, two, jnp.where(count > 0.5, 1.0 + low, 0.0)))
    choice[0] = case.astype(jnp.int32)

    for i in range(6):
        @pl.when(sides[i][0])
        def _():
            halo(i).wait_send()

    @pl.loop(1, GX)
    def _(k):
        outgoing(k).wait()


def pick(rows, anchors, d, c):
    k = anchors[2 * d + c]
    row = rows[jnp.minimum(k, 15)]
    return jnp.where(k < 16, row, jnp.zeros_like(row))


def second(dests, rows, anchors, recv, send, s_sem, r_sem):
    gx = lax.axis_index("gx")
    barrier = pltpu.get_barrier_semaphore()

    def copy(i, target, source):
        return pltpu.make_async_remote_copy(
            src_ref=send.at[i], dst_ref=recv.at[source], send_sem=s_sem.at[i], recv_sem=r_sem.at[source],
            device_id={"gx": target}, device_id_type=MESH,
        )

    hot = functools.reduce(jnp.logical_or, [gx == d for d in dests])

    @pl.when(hot)
    def _():
        @pl.loop(1, GX)
        def _(k):
            pl.semaphore_signal(barrier, inc=1, device_id={"gx": lax.rem(gx + k, GX)}, device_id_type=MESH)

    for i, d in enumerate(dests):
        send[i] = pick(rows, anchors, d, 1)
    pl.semaphore_wait(barrier, len(dests) - hot.astype(jnp.int32))
    for i, d in enumerate(dests):
        @pl.when(gx != d)
        def _():
            copy(i, d, gx).start()

        @pl.when(gx == d)
        def _():
            recv[gx] = send[i]

    @pl.when(jnp.logical_not(hot))
    def _():
        @pl.loop(0, GX)
        def _(s):
            recv[s] = jnp.zeros(recv.shape[1:], BF16)

    @pl.when(hot)
    def _():
        @pl.loop(1, GX)
        def _(k):
            s = lax.rem(gx + k, GX)
            copy(0, s, s).wait_recv()

    for i, d in enumerate(dests):
        @pl.when(gx != d)
        def _():
            copy(i, d, gx).wait_send()


def finish(one, two, out_hbm, out, sem):
    pi, qi = iota((256, 256), 0), iota((256, 256), 1)
    turn = ones_where((qi % 32 == pi // 8) & (qi // 32 == pi % 8))

    def store(b):
        return pltpu.make_async_copy(out.at[b], out_hbm.at[b], sem.at[b])

    @pl.loop(0, 11)
    def _(b):
        for g in range(2):
            parts = []
            for h in range(2):
                x = jnp.concatenate(
                    [ref[8 * g + 4 * h + s, b] for s in range(4) for ref in (one, two)], axis=0
                )
                parts.append(dot(turn, x).reshape(32, 8, 128))
            tile = jnp.concatenate(parts, axis=1).astype(BF16)
            for j in range(32):
                out[b, pl.ds(16 * g, 16), pl.ds(128 * j, 128)] = tile[j]
        store(b).start()

    @pl.loop(0, 11)
    def _(b):
        store(b).wait()


def local(a_blocks, prolong, pairing, route):
    a = a_blocks.reshape(4, 4, 2, 7, 32, 128).transpose(0, 1, 3, 4, 2, 5).reshape(16, 7, 64, 128)
    p = prolong.reshape(4, 4, 2, 32, 128).transpose(0, 1, 3, 2, 4).reshape(16, 64, 128)
    smem = pl.BlockSpec(memory_space=pltpu.SMEM)
    vmem = pl.BlockSpec(memory_space=pltpu.VMEM)
    hbm = pl.BlockSpec(memory_space=pltpu.HBM)
    row_set = jax.ShapeDtypeStruct((16, 11, 32, 128), BF16)
    one, rows, anchors, choice = pl.pallas_call(
        kernel,
        out_shape=(row_set, row_set, jax.ShapeDtypeStruct((32,), jnp.int32), jax.ShapeDtypeStruct((1,), jnp.int32)),
        in_specs=[smem, smem, hbm, hbm],
        out_specs=(vmem, vmem, smem, smem),
        scratch_shapes=[
            pltpu.VMEM((16, 7, 64, 128), BF16),
            pltpu.VMEM((16, 64, 128), BF16),
            pltpu.VMEM((4, 4, 64, 128), BF16),
            pltpu.VMEM((16, 64, 128), BF16),
            pltpu.VMEM((16, 128, 128), BF16),
            pltpu.VMEM((2, 4, 64, 128), BF16),
            pltpu.VMEM((2, 4, 64, 128), BF16),
            pltpu.VMEM((2, 8, 64, 128), BF16),
            pltpu.VMEM((2, 8, 64, 128), BF16),
            pltpu.VMEM((224, 32, 128), F32),
            pltpu.VMEM((16, 11, 32, 128), BF16),
            pltpu.VMEM((3, 8, 128), F32),
            pltpu.VMEM((GX, 8, 128), F32),
            pltpu.VMEM((GY, 8, 128), F32),
            pltpu.VMEM((GZ, 8, 128), F32),
            pltpu.SemaphoreType.DMA((2,)),
            pltpu.SemaphoreType.DMA((6,)),
            pltpu.SemaphoreType.DMA((6,)),
            pltpu.SemaphoreType.DMA((16,)),
            pltpu.SemaphoreType.DMA((16,)),
            pltpu.SemaphoreType.DMA((3, 16)),
            pltpu.SemaphoreType.DMA((3, 16)),
        ],
        compiler_params=pltpu.CompilerParams(
            collective_id=0, has_side_effects=True, vmem_limit_bytes=40 << 20
        ),
        cost_estimate=pl.CostEstimate(flops=1 << 30, bytes_accessed=8 << 20, transcendentals=0),
    )(pairing, route, a, p)

    def exchange(number):
        dests = CASES[number]
        if not dests:
            return lambda rows, anchors: jnp.zeros(row_set.shape, BF16)
        return pl.pallas_call(
            functools.partial(second, dests),
            out_shape=row_set,
            in_specs=[vmem, smem],
            out_specs=vmem,
            scratch_shapes=[
                pltpu.VMEM((len(dests), 11, 32, 128), BF16),
                pltpu.SemaphoreType.DMA((len(dests),)),
                pltpu.SemaphoreType.DMA((GX,)),
            ],
            compiler_params=pltpu.CompilerParams(
                collective_id=number, has_side_effects=True, vmem_limit_bytes=40 << 20
            ),
            cost_estimate=pl.CostEstimate(flops=0, bytes_accessed=4 << 20, transcendentals=0),
        )

    two = lax.switch(choice[0], [exchange(i) for i in range(len(CASES))], rows, anchors)

    out = pl.pallas_call(
        finish,
        out_shape=jax.ShapeDtypeStruct((11, 32, 4096), BF16),
        in_specs=[vmem, vmem],
        out_specs=hbm,
        scratch_shapes=[pltpu.VMEM((11, 32, 4096), BF16), pltpu.SemaphoreType.DMA((11,))],
        compiler_params=pltpu.CompilerParams(vmem_limit_bytes=40 << 20),
        cost_estimate=pl.CostEstimate(flops=1 << 30, bytes_accessed=6 << 20, transcendentals=0),
    )(one, two)
    return out.transpose(1, 0, 2)


def solution(mesh):
    placed = (
        P("gx", "gy", "gz", None, None),
        P("gx", "gy", "gz", None),
        P("gx", "gy", "gz"),
        P(("gx", "gy", "gz"), None),
    )
    return jax.shard_map(
        local,
        mesh=mesh,
        in_specs=placed,
        out_specs=P(("gx", "gy", "gz"), None, None),
        check_vma=False,
    )
```

```python
import functools

import jax
import jax.numpy as jnp
from jax import lax
from jax.experimental import pallas as pl
from jax.experimental.pallas import tpu as pltpu
from jax.sharding import PartitionSpec as P

MESH = pl.DeviceIdType.MESH
F32 = jnp.float32
BF16 = jnp.bfloat16
GX, GY, GZ = 16, 4, 4
AXES = (
    ("gx", GX, lambda: lax.axis_index("gx")),
    ("gy", GY, lambda: lax.axis_index("gy")),
    ("gz", GZ, lambda: lax.axis_index("gz")),
)
GROUPS = GX // 2
CASES = (
    [()]
    + [(g, g + GROUPS) for g in range(GROUPS)]
    + [(g, g + GROUPS, h, h + GROUPS) for g in range(GROUPS) for h in range(g + 1, GROUPS)]
    + [tuple(range(GX))]
)


def iota(shape, dim):
    return lax.broadcasted_iota(jnp.int32, shape, dim)


def ones_where(cond):
    return jnp.where(cond, 1.0, 0.0).astype(BF16)


def dot(a, b):
    return jnp.dot(a, b, preferred_element_type=F32)


def kernel(pair_hbm, route_hbm, a_hbm, p_hbm, recv, others, choice,
           pair_ref, route_ref, a_ref, p_ref, rows, anchors, nn, nr, ppt, hx, hy, hz, zs, gal, send, mine, seen_x, seen_y, seen_z,
           in_sem, hs_sem, hr_sem, s_sem, r_sem, fs_sem, fr_sem):
    gx, gy, gz = lax.axis_index("gx"), lax.axis_index("gy"), lax.axis_index("gz")

    load_p = pltpu.make_async_copy(p_hbm, p_ref, in_sem.at[0])
    load_a = pltpu.make_async_copy(a_hbm, a_ref, in_sem.at[1])
    load_route = pltpu.make_async_copy(route_hbm, route_ref, in_sem.at[2])
    load_pair = pltpu.make_async_copy(pair_hbm, pair_ref, in_sem.at[3])
    load_p.start()
    load_route.start()
    load_pair.start()
    load_a.start()
    barrier = pltpu.get_barrier_semaphore()
    for name, size, at in AXES:
        @pl.loop(1, size)
        def _(k):
            pl.semaphore_signal(barrier, inc=1, device_id={name: lax.rem(at() + k, size)}, device_id_type=MESH)
    sides = (
        (gx > 0, {"gx": gx - 1}), (gx < GX - 1, {"gx": gx + 1}),
        (gy > 0, {"gy": gy - 1}), (gy < GY - 1, {"gy": gy + 1}),
        (gz > 0, {"gz": gz - 1}), (gz < GZ - 1, {"gz": gz + 1}),
    )
    left = iota((64, 128), 1) < 64

    ci, ki = iota((64, 128), 0), iota((64, 128), 1)
    order = ones_where(((ki // 2) % 32 == ci // 2) & (ki // 64 == (ci + ki) % 2))
    ri, li = iota((128, 128), 0), iota((128, 128), 1)
    spread = ones_where(li % 64 == 2 * (ri % 32) + (ri // 32) % 2)
    same_z = li % 2 == ri // 64
    z_lane = (ri % 2) == (li // 64)
    half_row = (ri // 64) == (li // 64)

    def prepare(i, carry):
        for u in range(2):
            xy = 2 * i + u
            raw = p_ref[xy].astype(F32)
            both = jnp.concatenate([raw, pltpu.roll(raw, 64, 1)], axis=0)
            tile = dot(order, jnp.where(z_lane, both, 0.0).astype(BF16))
            nn[xy // 4, xy % 4] = tile.astype(BF16)
            turned = pltpu.roll(tile, 64, 1)
            nr[xy] = turned.astype(BF16)
            twice = jnp.concatenate([raw, raw], axis=0)
            twice = jnp.where(half_row, twice, 0.0).astype(BF16)
            t = lax.dot_general(spread, twice, (((1,), (1,)), ((), ())), preferred_element_type=F32)
            ppt[xy] = jnp.where(same_z, t, 0.0).astype(BF16)
            if u == 0:
                low, high = tile, turned
            else:
                zs[0, i] = jnp.where(left, low, turned).astype(BF16)
                zs[1, i] = jnp.where(left, high, tile).astype(BF16)
        return carry

    load_p.wait()
    lax.fori_loop(0, 8, prepare, 0)

    lane = iota((8, 128), 1)

    def anchor(d, flags):
        def look(k, state):
            one, two = state
            hit = route_ref[k] == d
            two = jnp.where(hit & (one < 16) & (two == 16), k, two)
            one = jnp.where(hit & (one == 16), k, one)
            return one, two

        one, two = lax.fori_loop(0, 16, look, (jnp.int32(16), jnp.int32(16)))
        anchors[2 * d] = one
        anchors[2 * d + 1] = two
        return jnp.where((lane == d) & (two < 16), 1.0, flags)

    load_route.wait()
    mine[0] = lax.fori_loop(0, GX, anchor, jnp.zeros((8, 128), F32))
    pl.semaphore_wait(barrier, GX + GY + GZ - 3)

    def tell(stage, k, seen):
        name, size, at = AXES[stage]
        return pltpu.make_async_remote_copy(
            src_ref=mine.at[stage], dst_ref=seen.at[k], send_sem=fs_sem.at[stage, k], recv_sem=fr_sem.at[stage, k],
            device_id={name: lax.rem(at() + k, size)}, device_id_type=MESH,
        )

    stages = (seen_x, seen_y, seen_z)

    def tell_all(stage):
        for k in range(1, AXES[stage][1]):
            tell(stage, k, stages[stage]).start()

    def hear_all(stage):
        flags = mine[stage]
        for k in range(1, AXES[stage][1]):
            tell(stage, k, stages[stage]).wait()
            flags = jnp.maximum(flags, stages[stage][k])
        return flags

    faces = (
        (nn.at[0], hx.at[1]), (nn.at[3], hx.at[0]),
        (nn.at[:, 0], hy.at[1]), (nn.at[:, 3], hy.at[0]),
        (zs.at[0], hz.at[1]), (zs.at[1], hz.at[0]),
    )
    own_halo = (hx.at[0], hx.at[1], hy.at[0], hy.at[1], hz.at[0], hz.at[1])

    def halo(i):
        source, target = faces[i]
        return pltpu.make_async_remote_copy(
            src_ref=source, dst_ref=target, send_sem=hs_sem.at[i], recv_sem=hr_sem.at[i],
            device_id=sides[i][1], device_id_type=MESH,
        )

    for i in range(6):
        @pl.when(sides[i][0])
        def _():
            halo(i).start()

        @pl.when(jnp.logical_not(sides[i][0]))
        def _():
            own_halo[i][...] = jnp.zeros(own_halo[i].shape, BF16)

    tell_all(0)
    load_a.wait()
    load_pair.wait()
    zero = jnp.zeros((64, 128), BF16)
    left32 = iota((32, 128), 1) < 64

    def product(xy, s, near_tile):
        wide = jnp.concatenate(
            [jnp.concatenate([near_tile, zero], axis=1), jnp.concatenate([zero, near_tile], axis=1)], axis=0
        )
        mixed = dot(a_ref[xy, s], wide).astype(BF16)
        mixed = jnp.concatenate([mixed[:, :128], mixed[:, 128:]], axis=0)
        g = dot(ppt[xy], mixed)
        gal[xy * 14 + 2 * s] = jnp.where(left32, g[0:32], pltpu.roll(g[32:64], 64, 1))
        gal[xy * 14 + 2 * s + 1] = jnp.where(left32, pltpu.roll(g[64:96], 64, 1), g[96:128])

    def loop(n, body):
        def step(i, carry):
            body(i)
            return carry
        lax.fori_loop(0, n, step, 0)

    @pl.loop(0, 4)
    def _(x):
        for y in range(4):
            product(x * 4 + y, 0, nn[x, y])

    @pl.loop(0, 3)
    def _(i):
        for k in range(4):
            product(i * 4 + 4 + k, 1, nn[i, k])
            product(i * 4 + k, 2, nn[i + 1, k])

    @pl.loop(0, 3)
    def _(i):
        for k in range(4):
            product(k * 4 + i + 1, 3, nn[k, i])
            product(k * 4 + i, 4, nn[k, i + 1])

    mine[1] = hear_all(0)
    tell_all(1)

    for i in range(6):
        @pl.when(sides[i][0])
        def _():
            j = i ^ 1
            source, target = faces[j]
            pltpu.make_async_remote_copy(
                src_ref=source, dst_ref=target, send_sem=hs_sem.at[j], recv_sem=hr_sem.at[j],
                device_id=sides[i][1], device_id_type=MESH,
            ).wait_recv()

    @pl.loop(0, 4)
    def _(k):
        product(k, 1, hx[0, k])
        product(12 + k, 2, hx[1, k])
        product(k * 4, 3, hy[0, k])
        product(k * 4 + 3, 4, hy[1, k])

    @pl.loop(0, 8)
    def _(q):
        below, above = hz[0, q].astype(F32), hz[1, q].astype(F32)
        below = (below, pltpu.roll(below, 64, 1))
        above = (pltpu.roll(above, 64, 1), above)
        for u in range(2):
            xy = 2 * q + u
            own = nr[xy]
            product(xy, 5, jnp.where(left, below[u].astype(BF16), own))
            product(xy, 6, jnp.where(left, own, above[u].astype(BF16)))

    mine[2] = hear_all(1)
    tell_all(2)

    @pl.loop(0, 16)
    def _(k):
        a, b, z, t = k // 8, (k // 4) % 2, (k // 2) % 2, k % 2
        along = pair_ref[a, b, z] == 0
        corner = a * 8 + b * 2
        first = jnp.where(along, corner + t, corner + 4 * t)
        second = jnp.where(along, corner + 4 + t, corner + 4 * t + 1)

        def block(xy, s):
            return gal[xy * 14 + 2 * s + z]

        rows[k, 0] = (
            block(first, 0) + block(second, 0)
            + block(first, jnp.where(along, 2, 4)) + block(second, jnp.where(along, 1, 3))
        ).astype(BF16)
        slots_x = ((1, 3, 4, 5, 6), (2, 3, 4, 5, 6))
        slots_y = ((1, 2, 3, 5, 6), (1, 2, 4, 5, 6))
        for i, xy in enumerate((first, second)):
            for j in range(5):
                rows[k, 1 + 5 * i + j] = block(xy, jnp.where(along, slots_x[i][j], slots_y[i][j])).astype(BF16)

    def outgoing(k):
        return pltpu.make_async_remote_copy(
            src_ref=send.at[k], dst_ref=recv.at[gx], send_sem=s_sem.at[k], recv_sem=r_sem.at[k],
            device_id={"gx": lax.rem(gx + k, GX)}, device_id_type=MESH,
        )

    @pl.loop(1, GX)
    def _(k):
        send[k] = pick(rows, anchors, lax.rem(gx + k, GX), 0)
        outgoing(k).start()

    recv[gx] = pick(rows, anchors, gx, 0)

    @pl.loop(0, GX)
    def _(d):
        others[d] = pick(rows, anchors, d, 1)

    flags = hear_all(2)[0:1]
    flags = jnp.maximum(flags, pltpu.roll(flags, 128 - GROUPS, 1))
    flags = jnp.where(iota((1, 128), 1) < GROUPS, flags, 0.0)
    place = iota((1, 128), 1).astype(F32)
    count = jnp.sum(flags)
    high = jnp.max(jnp.where(flags > 0, place, 0.0))
    low = jnp.min(jnp.where(flags > 0, place, 128.0))
    two = 1.0 + GROUPS + low * (2 * GROUPS - 1 - low) * 0.5 + (high - low - 1.0)
    case = jnp.where(count > 2.5, 1.0 * (len(CASES) - 1), jnp.where(count > 1.5, two, jnp.where(count > 0.5, 1.0 + low, 0.0)))
    choice[0] = case.astype(jnp.int32)
    choice[1] = (jnp.sum(jnp.where(place == lax.rem(gx, GROUPS).astype(F32), flags, 0.0)) > 0.5).astype(jnp.int32)

    for i in range(6):
        @pl.when(sides[i][0])
        def _():
            halo(i).wait_send()

    @pl.loop(1, GX)
    def _(k):
        outgoing(k).wait()


def pick(rows, anchors, d, c):
    k = anchors[2 * d + c]
    row = rows[jnp.minimum(k, 15)]
    return jnp.where(k < 16, row, jnp.zeros_like(row))


def second(dests, rows, recv, s_sem, r_sem):
    gx = lax.axis_index("gx")
    barrier = pltpu.get_barrier_semaphore()
    number = len(dests)
    hot = functools.reduce(jnp.logical_or, [gx == d for d in dests]) if number < GX else gx >= 0

    @pl.when(hot)
    def _():
        @pl.loop(1, GX)
        def _(k):
            pl.semaphore_signal(barrier, inc=1, device_id={"gx": lax.rem(gx + k, GX)}, device_id_type=MESH)

    def copy(source, target, device):
        return pltpu.make_async_remote_copy(
            src_ref=source, dst_ref=target, send_sem=s_sem, recv_sem=r_sem,
            device_id={"gx": device}, device_id_type=MESH,
        )

    def bytes_of(n):
        return copy(rows.at[pl.ds(0, n)], recv.at[pl.ds(0, n)], 0)

    pl.semaphore_wait(barrier, number - hot.astype(jnp.int32))

    @pl.loop(0, number)
    def _(i):
        if number == GX:
            d = lax.rem(gx + i, GX)
        else:
            d = dests[0] + GROUPS * lax.rem(i, 2)
            d = jnp.where(i < 2, d, d + dests[-2] - dests[0])

        @pl.when(gx != d)
        def _():
            copy(rows.at[d], recv.at[gx], d).start()

    @pl.when(hot)
    def _():
        bytes_of(GX - 1).wait_recv()
        bytes_of(number - 1).wait_send()

    @pl.when(jnp.logical_not(hot))
    def _():
        bytes_of(number).wait_send()


def finish(choice, one, two, own, out_hbm, out, sem):
    hot, gx = choice[1] == 1, lax.axis_index("gx")
    pi, qi = iota((256, 256), 0), iota((256, 256), 1)
    turn = ones_where((qi % 32 == pi // 8) & (qi // 32 == pi % 8))

    def store(b):
        return pltpu.make_async_copy(out.at[b], out_hbm.at[b], sem.at[b])

    @pl.loop(0, 11)
    def _(b):
        for g in range(2):
            parts = []
            for h in range(2):
                x = []
                for s in range(8 * g + 4 * h, 8 * g + 4 * h + 4):
                    late = jnp.where(gx == s, own[gx, b], two[s, b])
                    x += [one[s, b], jnp.where(hot, late, jnp.zeros_like(late))]
                x = jnp.concatenate(x, axis=0)
                parts.append(dot(turn, x).reshape(32, 8, 128))
            tile = jnp.concatenate(parts, axis=1).astype(BF16)
            for j in range(32):
                out[b, pl.ds(16 * g, 16), pl.ds(128 * j, 128)] = tile[j]
        store(b).start()

    @pl.loop(0, 11)
    def _(b):
        store(b).wait()


def local(a_blocks, prolong, pairing, route):
    a = a_blocks.reshape(4, 4, 2, 7, 32, 128).transpose(0, 1, 3, 4, 2, 5).reshape(16, 7, 64, 128)
    p = prolong.reshape(4, 4, 2, 32, 128).transpose(0, 1, 3, 2, 4).reshape(16, 64, 128)
    smem = pl.BlockSpec(memory_space=pltpu.SMEM)
    vmem = pl.BlockSpec(memory_space=pltpu.VMEM)
    hbm = pl.BlockSpec(memory_space=pltpu.HBM)
    row_set = jax.ShapeDtypeStruct((16, 11, 32, 128), BF16)
    one, others, choice = pl.pallas_call(
        kernel,
        out_shape=(row_set, row_set, jax.ShapeDtypeStruct((2,), jnp.int32)),
        in_specs=[hbm, hbm, hbm, hbm],
        out_specs=(vmem, vmem, smem),
        scratch_shapes=[
            pltpu.SMEM((2, 2, 2), jnp.int32),
            pltpu.SMEM((16,), jnp.int32),
            pltpu.VMEM((16, 7, 64, 128), BF16),
            pltpu.VMEM((16, 64, 128), BF16),
            pltpu.VMEM((16, 11, 32, 128), BF16),
            pltpu.SMEM((32,), jnp.int32),
            pltpu.VMEM((4, 4, 64, 128), BF16),
            pltpu.VMEM((16, 64, 128), BF16),
            pltpu.VMEM((16, 128, 128), BF16),
            pltpu.VMEM((2, 4, 64, 128), BF16),
            pltpu.VMEM((2, 4, 64, 128), BF16),
            pltpu.VMEM((2, 8, 64, 128), BF16),
            pltpu.VMEM((2, 8, 64, 128), BF16),
            pltpu.VMEM((224, 32, 128), F32),
            pltpu.VMEM((16, 11, 32, 128), BF16),
            pltpu.VMEM((3, 8, 128), F32),
            pltpu.VMEM((GX, 8, 128), F32),
            pltpu.VMEM((GY, 8, 128), F32),
            pltpu.VMEM((GZ, 8, 128), F32),
            pltpu.SemaphoreType.DMA((4,)),
            pltpu.SemaphoreType.DMA((6,)),
            pltpu.SemaphoreType.DMA((6,)),
            pltpu.SemaphoreType.DMA((16,)),
            pltpu.SemaphoreType.DMA((16,)),
            pltpu.SemaphoreType.DMA((3, 16)),
            pltpu.SemaphoreType.DMA((3, 16)),
        ],
        compiler_params=pltpu.CompilerParams(
            collective_id=0, has_side_effects=True, vmem_limit_bytes=60 << 20
        ),
        cost_estimate=pl.CostEstimate(flops=1 << 30, bytes_accessed=8 << 20, transcendentals=0),
    )(pairing, route.reshape(16), a, p)

    def exchange(number):
        dests = CASES[number]
        if not dests:
            return lambda rows: rows
        return pl.pallas_call(
            functools.partial(second, dests),
            out_shape=row_set,
            in_specs=[vmem],
            out_specs=vmem,
            scratch_shapes=[
                pltpu.SemaphoreType.DMA,
                pltpu.SemaphoreType.DMA,
            ],
            compiler_params=pltpu.CompilerParams(
                collective_id=number, has_side_effects=True, vmem_limit_bytes=40 << 20
            ),
            cost_estimate=pl.CostEstimate(flops=0, bytes_accessed=4 << 20, transcendentals=0),
        )

    two = lax.switch(choice[0], [exchange(i) for i in range(len(CASES))], others)

    out = pl.pallas_call(
        finish,
        out_shape=jax.ShapeDtypeStruct((11, 32, 4096), BF16),
        in_specs=[smem, vmem, vmem, vmem],
        out_specs=hbm,
        scratch_shapes=[pltpu.VMEM((11, 32, 4096), BF16), pltpu.SemaphoreType.DMA((11,))],
        compiler_params=pltpu.CompilerParams(vmem_limit_bytes=40 << 20),
        cost_estimate=pl.CostEstimate(flops=1 << 30, bytes_accessed=6 << 20, transcendentals=0),
    )(choice, one, two, others)
    return out.transpose(1, 0, 2)


def solution(mesh):
    placed = (
        P("gx", "gy", "gz", None, None),
        P("gx", "gy", "gz", None),
        P("gx", "gy", "gz"),
        P(("gx", "gy", "gz"), None),
    )
    return jax.shard_map(
        local,
        mesh=mesh,
        in_specs=placed,
        out_specs=P(("gx", "gy", "gz"), None, None),
        check_vma=False,
    )
```

```python
import functools

import jax
import jax.numpy as jnp
from jax import lax
from jax.experimental import pallas as pl
from jax.experimental.pallas import tpu as pltpu
from jax.sharding import PartitionSpec as P

MESH = pl.DeviceIdType.MESH
F32 = jnp.float32
BF16 = jnp.bfloat16
GX, GY, GZ = 16, 4, 4
AXES = (
    ("gx", GX, lambda: lax.axis_index("gx")),
    ("gy", GY, lambda: lax.axis_index("gy")),
    ("gz", GZ, lambda: lax.axis_index("gz")),
)
GROUPS = GX // 2
CASES = (
    [()]
    + [(g, g + GROUPS) for g in range(GROUPS)]
    + [(g, g + GROUPS, h, h + GROUPS) for g in range(GROUPS) for h in range(g + 1, GROUPS)]
    + [tuple(range(GX))]
)


def iota(shape, dim):
    return lax.broadcasted_iota(jnp.int32, shape, dim)


def ones_where(cond):
    return jnp.where(cond, 1.0, 0.0).astype(BF16)


def dot(a, b):
    return jnp.dot(a, b, preferred_element_type=F32)


def kernel(pair_hbm, route_hbm, a_hbm, p_hbm, recv, others, choice,
           pair_ref, route_ref, a_ref, p_ref, rows, anchors, nn, nr, ppt, hx, hy, hz, zs, gal, send, mine, seen_x, seen_y, seen_z,
           in_sem, hs_sem, hr_sem, s_sem, r_sem, fs_sem, fr_sem):
    gx, gy, gz = lax.axis_index("gx"), lax.axis_index("gy"), lax.axis_index("gz")

    load_p = pltpu.make_async_copy(p_hbm, p_ref, in_sem.at[0])
    load_a = pltpu.make_async_copy(a_hbm, a_ref, in_sem.at[1])
    load_route = pltpu.make_async_copy(route_hbm, route_ref, in_sem.at[2])
    load_pair = pltpu.make_async_copy(pair_hbm, pair_ref, in_sem.at[3])
    load_p.start()
    load_route.start()
    load_pair.start()
    load_a.start()
    barrier = pltpu.get_barrier_semaphore()
    for name, size, at in AXES:
        @pl.loop(1, size)
        def _(k):
            pl.semaphore_signal(barrier, inc=1, device_id={name: lax.rem(at() + k, size)}, device_id_type=MESH)
    sides = (
        (gx > 0, {"gx": gx - 1}), (gx < GX - 1, {"gx": gx + 1}),
        (gy > 0, {"gy": gy - 1}), (gy < GY - 1, {"gy": gy + 1}),
        (gz > 0, {"gz": gz - 1}), (gz < GZ - 1, {"gz": gz + 1}),
    )
    left = iota((64, 128), 1) < 64

    ci, ki = iota((64, 128), 0), iota((64, 128), 1)
    order = ones_where(((ki // 2) % 32 == ci // 2) & (ki // 64 == (ci + ki) % 2))
    ri, li = iota((128, 128), 0), iota((128, 128), 1)
    spread = ones_where(li % 64 == 2 * (ri % 32) + (ri // 32) % 2)
    same_z = li % 2 == ri // 64
    z_lane = (ri % 2) == (li // 64)
    half_row = (ri // 64) == (li // 64)

    def prepare(i, carry):
        for u in range(2):
            xy = 2 * i + u
            raw = p_ref[xy].astype(F32)
            both = jnp.concatenate([raw, pltpu.roll(raw, 64, 1)], axis=0)
            tile = dot(order, jnp.where(z_lane, both, 0.0).astype(BF16))
            nn[xy // 4, xy % 4] = tile.astype(BF16)
            turned = pltpu.roll(tile, 64, 1)
            nr[xy] = turned.astype(BF16)
            twice = jnp.concatenate([raw, raw], axis=0)
            twice = jnp.where(half_row, twice, 0.0).astype(BF16)
            t = lax.dot_general(spread, twice, (((1,), (1,)), ((), ())), preferred_element_type=F32)
            ppt[xy] = jnp.where(same_z, t, 0.0).astype(BF16)
            if u == 0:
                low, high = tile, turned
            else:
                zs[0, i] = jnp.where(left, low, turned).astype(BF16)
                zs[1, i] = jnp.where(left, high, tile).astype(BF16)
        return carry

    load_p.wait()
    lax.fori_loop(0, 8, prepare, 0)

    pl.semaphore_wait(barrier, GX + GY + GZ - 3)

    def tell(stage, k, seen):
        name, size, at = AXES[stage]
        return pltpu.make_async_remote_copy(
            src_ref=mine.at[stage], dst_ref=seen.at[k], send_sem=fs_sem.at[stage, k], recv_sem=fr_sem.at[stage, k],
            device_id={name: lax.rem(at() + k, size)}, device_id_type=MESH,
        )

    stages = (seen_x, seen_y, seen_z)

    def tell_all(stage):
        for k in range(1, AXES[stage][1]):
            tell(stage, k, stages[stage]).start()

    def hear_all(stage):
        flags = mine[stage]
        for k in range(1, AXES[stage][1]):
            tell(stage, k, stages[stage]).wait()
            flags = jnp.maximum(flags, stages[stage][k])
        return flags

    faces = (
        (nn.at[0], hx.at[1]), (nn.at[3], hx.at[0]),
        (nn.at[:, 0], hy.at[1]), (nn.at[:, 3], hy.at[0]),
        (zs.at[0], hz.at[1]), (zs.at[1], hz.at[0]),
    )
    own_halo = (hx.at[0], hx.at[1], hy.at[0], hy.at[1], hz.at[0], hz.at[1])

    def halo(i):
        source, target = faces[i]
        return pltpu.make_async_remote_copy(
            src_ref=source, dst_ref=target, send_sem=hs_sem.at[i], recv_sem=hr_sem.at[i],
            device_id=sides[i][1], device_id_type=MESH,
        )

    for i in (4, 5, 0, 1, 2, 3):
        @pl.when(sides[i][0])
        def _():
            halo(i).start()

        @pl.when(jnp.logical_not(sides[i][0]))
        def _():
            own_halo[i][...] = jnp.zeros(own_halo[i].shape, BF16)

    lane = iota((8, 128), 1)

    def anchor(d, flags):
        def look(k, state):
            one, two = state
            hit = route_ref[k] == d
            two = jnp.where(hit & (one < 16) & (two == 16), k, two)
            one = jnp.where(hit & (one == 16), k, one)
            return one, two

        one, two = lax.fori_loop(0, 16, look, (jnp.int32(16), jnp.int32(16)), unroll=True)
        anchors[2 * d] = one
        anchors[2 * d + 1] = two
        return jnp.where((lane == d) & (two < 16), 1.0, flags)

    load_route.wait()
    mine[0] = lax.fori_loop(0, GX, anchor, jnp.zeros((8, 128), F32))
    tell_all(0)
    load_a.wait()
    load_pair.wait()
    zero = jnp.zeros((64, 128), BF16)
    left32 = iota((32, 128), 1) < 64

    def mix(xy, s, near_tile):
        wide = jnp.concatenate(
            [jnp.concatenate([near_tile, zero], axis=1), jnp.concatenate([zero, near_tile], axis=1)], axis=0
        )
        mixed = dot(a_ref[xy, s], wide).astype(BF16)
        return jnp.concatenate([mixed[:, :128], mixed[:, 128:]], axis=0)

    def keep(xy, s, g):
        gal[xy * 14 + 2 * s] = jnp.where(left32, g[0:32], pltpu.roll(g[32:64], 64, 1))
        gal[xy * 14 + 2 * s + 1] = jnp.where(left32, pltpu.roll(g[64:96], 64, 1), g[96:128])

    def product(xy, s, near_tile):
        keep(xy, s, dot(ppt[xy], mix(xy, s, near_tile)))

    def products(xy, s, t, near_s, near_t):
        g = dot(ppt[xy], jnp.concatenate([mix(xy, s, near_s), mix(xy, t, near_t)], axis=1))
        keep(xy, s, g[:, :128])
        keep(xy, t, g[:, 128:])

    @pl.loop(0, 4)
    def _(x):
        for y in range(4):
            product(x * 4 + y, 0, nn[x, y])

    @pl.loop(0, 3)
    def _(i):
        for k in range(4):
            product(i * 4 + 4 + k, 1, nn[i, k])
            product(i * 4 + k, 2, nn[i + 1, k])

    def arrived(i):
        @pl.when(sides[i][0])
        def _():
            j = i ^ 1
            source, target = faces[j]
            pltpu.make_async_remote_copy(
                src_ref=source, dst_ref=target, send_sem=hs_sem.at[j], recv_sem=hr_sem.at[j],
                device_id=sides[i][1], device_id_type=MESH,
            ).wait_recv()

    arrived(4)
    arrived(5)

    @pl.loop(0, 8)
    def _(q):
        below, above = hz[0, q].astype(F32), hz[1, q].astype(F32)
        below = (below, pltpu.roll(below, 64, 1))
        above = (pltpu.roll(above, 64, 1), above)
        for u in range(2):
            xy = 2 * q + u
            own = nr[xy]
            products(xy, 5, 6, jnp.where(left, below[u].astype(BF16), own), jnp.where(left, own, above[u].astype(BF16)))

    def place_of(k):
        a, b, z, t = k // 8, (k // 4) % 2, (k // 2) % 2, k % 2
        along = pair_ref[a, b, z] == 0
        corner = a * 8 + b * 2
        first = jnp.where(along, corner + t, corner + 4 * t)
        second = jnp.where(along, corner + 4 + t, corner + 4 * t + 1)
        return along, first, second, lambda xy, s: gal[xy * 14 + 2 * s + z]

    @pl.loop(0, 16)
    def _(k):
        along, first, second, block = place_of(k)
        for i, xy in enumerate((first, second)):
            for j in range(2):
                rows[k, 2 * i + j] = block(xy, 5 + j).astype(BF16)

    parts = (pl.ds(0, 4), pl.ds(4, 7))

    def outgoing(part, k):
        return pltpu.make_async_remote_copy(
            src_ref=send.at[k, parts[part]], dst_ref=recv.at[gx, parts[part]],
            send_sem=s_sem.at[part, k], recv_sem=r_sem.at[part, k],
            device_id={"gx": lax.rem(gx + k, GX)}, device_id_type=MESH,
        )

    def post(part):
        @pl.loop(1, GX)
        def _(k):
            send[k, parts[part]] = pick(rows, anchors, lax.rem(gx + k, GX), 0, parts[part])
            outgoing(part, k).start()

    post(0)

    @pl.loop(0, 3)
    def _(i):
        for k in range(4):
            product(k * 4 + i + 1, 3, nn[k, i])
            product(k * 4 + i, 4, nn[k, i + 1])

    mine[1] = hear_all(0)
    tell_all(1)
    for i in range(4):
        arrived(i)

    @pl.loop(0, 4)
    def _(k):
        product(k, 1, hx[0, k])
        product(12 + k, 2, hx[1, k])
        product(k * 4, 3, hy[0, k])
        product(k * 4 + 3, 4, hy[1, k])

    mine[2] = hear_all(1)
    tell_all(2)

    @pl.loop(0, 16)
    def _(k):
        along, first, second, block = place_of(k)
        rows[k, 4] = (
            block(first, 0) + block(second, 0)
            + block(first, jnp.where(along, 2, 4)) + block(second, jnp.where(along, 1, 3))
        ).astype(BF16)
        slots_x = ((1, 3, 4), (2, 3, 4))
        slots_y = ((1, 2, 3), (1, 2, 4))
        for i, xy in enumerate((first, second)):
            for j in range(3):
                rows[k, 5 + 3 * i + j] = block(xy, jnp.where(along, slots_x[i][j], slots_y[i][j])).astype(BF16)

    post(1)
    recv[gx] = pick(rows, anchors, gx, 0)

    @pl.loop(0, GX)
    def _(d):
        others[d] = pick(rows, anchors, d, 1)

    flags = hear_all(2)[0:1]
    flags = jnp.maximum(flags, pltpu.roll(flags, 128 - GROUPS, 1))
    flags = jnp.where(iota((1, 128), 1) < GROUPS, flags, 0.0)
    place = iota((1, 128), 1).astype(F32)
    count = jnp.sum(flags)
    high = jnp.max(jnp.where(flags > 0, place, 0.0))
    low = jnp.min(jnp.where(flags > 0, place, 128.0))
    two = 1.0 + GROUPS + low * (2 * GROUPS - 1 - low) * 0.5 + (high - low - 1.0)
    case = jnp.where(count > 2.5, 1.0 * (len(CASES) - 1), jnp.where(count > 1.5, two, jnp.where(count > 0.5, 1.0 + low, 0.0)))
    choice[0] = case.astype(jnp.int32)
    choice[1] = (jnp.sum(jnp.where(place == lax.rem(gx, GROUPS).astype(F32), flags, 0.0)) > 0.5).astype(jnp.int32)

    for i in range(6):
        @pl.when(sides[i][0])
        def _():
            halo(i).wait_send()

    @pl.loop(1, GX)
    def _(k):
        outgoing(0, k).wait()
        outgoing(1, k).wait()


def pick(rows, anchors, d, c, part=slice(None)):
    k = anchors[2 * d + c]
    row = rows[jnp.minimum(k, 15), part]
    return jnp.where(k < 16, row, jnp.zeros_like(row))


def second(dests, rows, recv, s_sem, r_sem, own_sem):
    gx = lax.axis_index("gx")
    barrier = pltpu.get_barrier_semaphore()
    number = len(dests)
    hot = functools.reduce(jnp.logical_or, [gx == d for d in dests]) if number < GX else gx >= 0

    @pl.when(hot)
    def _():
        @pl.loop(1, GX)
        def _(k):
            pl.semaphore_signal(barrier, inc=1, device_id={"gx": lax.rem(gx + k, GX)}, device_id_type=MESH)

    def copy(source, target, device):
        return pltpu.make_async_remote_copy(
            src_ref=source, dst_ref=target, send_sem=s_sem, recv_sem=r_sem,
            device_id={"gx": device}, device_id_type=MESH,
        )

    def bytes_of(n):
        return copy(rows.at[pl.ds(0, n)], recv.at[pl.ds(0, n)], 0)

    pl.semaphore_wait(barrier, number - hot.astype(jnp.int32))

    @pl.loop(0, number)
    def _(i):
        if number == GX:
            d = lax.rem(gx + i, GX)
        else:
            d = dests[0] + GROUPS * lax.rem(i, 2)
            d = jnp.where(i < 2, d, d + dests[-2] - dests[0])

        @pl.when(gx != d)
        def _():
            copy(rows.at[d], recv.at[gx], d).start()

    @pl.when(hot)
    def _():
        own = pltpu.make_async_copy(rows.at[gx], recv.at[gx], own_sem)
        own.start()
        own.wait()
        bytes_of(GX - 1).wait_recv()
        bytes_of(number - 1).wait_send()

    @pl.when(jnp.logical_not(hot))
    def _():
        bytes_of(number).wait_send()


def finish(choice, one, two, out_hbm, out, sem):
    pi, qi = iota((256, 256), 0), iota((256, 256), 1)
    turn = ones_where((qi % 32 == pi // 8) & (qi // 32 == pi % 8))
    zero = jnp.zeros((32, 128), BF16)

    def store(b):
        return pltpu.make_async_copy(out.at[b], out_hbm.at[b], sem.at[b])

    def turned(hot):
        @pl.loop(0, 11)
        def _(i):
            b = jnp.where(i < 4, 4 + i % 2 + 5 * (i // 2), jnp.where(i < 8, i - 4, i - 2))
            for g in range(2):
                x = [
                    jnp.concatenate(
                        [t for s in range(4) for t in (one[8 * g + 4 * h + s, i], two[8 * g + 4 * h + s, i] if hot else zero)],
                        axis=0,
                    )
                    for h in range(2)
                ]
                y = dot(turn, jnp.concatenate(x, axis=1))
                tile = jnp.concatenate([y[:, :128].reshape(32, 8, 128), y[:, 128:].reshape(32, 8, 128)], axis=1).astype(BF16)
                for j in range(32):
                    out[b, pl.ds(16 * g, 16), pl.ds(128 * j, 128)] = tile[j]
            store(b).start()

    pl.when(choice[1] == 1)(lambda: turned(True))
    pl.when(choice[1] != 1)(lambda: turned(False))

    @pl.loop(0, 11)
    def _(b):
        store(b).wait()


def local(a_blocks, prolong, pairing, route):
    a = a_blocks.reshape(4, 4, 2, 7, 32, 128).transpose(0, 1, 3, 4, 2, 5).reshape(16, 7, 64, 128)
    p = prolong.reshape(4, 4, 2, 32, 128).transpose(0, 1, 3, 2, 4).reshape(16, 64, 128)
    smem = pl.BlockSpec(memory_space=pltpu.SMEM)
    vmem = pl.BlockSpec(memory_space=pltpu.VMEM)
    hbm = pl.BlockSpec(memory_space=pltpu.HBM)
    row_set = jax.ShapeDtypeStruct((16, 11, 32, 128), BF16)
    one, others, choice = pl.pallas_call(
        kernel,
        out_shape=(row_set, row_set, jax.ShapeDtypeStruct((2,), jnp.int32)),
        in_specs=[hbm, hbm, hbm, hbm],
        out_specs=(vmem, vmem, smem),
        scratch_shapes=[
            pltpu.SMEM((2, 2, 2), jnp.int32),
            pltpu.SMEM((16,), jnp.int32),
            pltpu.VMEM((16, 7, 64, 128), BF16),
            pltpu.VMEM((16, 64, 128), BF16),
            pltpu.VMEM((16, 11, 32, 128), BF16),
            pltpu.SMEM((32,), jnp.int32),
            pltpu.VMEM((4, 4, 64, 128), BF16),
            pltpu.VMEM((16, 64, 128), BF16),
            pltpu.VMEM((16, 128, 128), BF16),
            pltpu.VMEM((2, 4, 64, 128), BF16),
            pltpu.VMEM((2, 4, 64, 128), BF16),
            pltpu.VMEM((2, 8, 64, 128), BF16),
            pltpu.VMEM((2, 8, 64, 128), BF16),
            pltpu.VMEM((224, 32, 128), F32),
            pltpu.VMEM((16, 11, 32, 128), BF16),
            pltpu.VMEM((3, 8, 128), F32),
            pltpu.VMEM((GX, 8, 128), F32),
            pltpu.VMEM((GY, 8, 128), F32),
            pltpu.VMEM((GZ, 8, 128), F32),
            pltpu.SemaphoreType.DMA((4,)),
            pltpu.SemaphoreType.DMA((6,)),
            pltpu.SemaphoreType.DMA((6,)),
            pltpu.SemaphoreType.DMA((2, 16)),
            pltpu.SemaphoreType.DMA((2, 16)),
            pltpu.SemaphoreType.DMA((3, 16)),
            pltpu.SemaphoreType.DMA((3, 16)),
        ],
        compiler_params=pltpu.CompilerParams(
            collective_id=0, has_side_effects=True, vmem_limit_bytes=60 << 20
        ),
        cost_estimate=pl.CostEstimate(flops=1 << 30, bytes_accessed=8 << 20, transcendentals=0),
    )(pairing, route.reshape(16), a, p)

    def exchange(number):
        dests = CASES[number]
        if not dests:
            return lambda rows: rows
        return pl.pallas_call(
            functools.partial(second, dests),
            out_shape=row_set,
            in_specs=[vmem],
            out_specs=vmem,
            scratch_shapes=[
                pltpu.SemaphoreType.DMA,
                pltpu.SemaphoreType.DMA,
                pltpu.SemaphoreType.DMA,
            ],
            compiler_params=pltpu.CompilerParams(
                collective_id=number, has_side_effects=True, vmem_limit_bytes=40 << 20
            ),
            cost_estimate=pl.CostEstimate(flops=0, bytes_accessed=4 << 20, transcendentals=0),
        )

    two = lax.switch(choice[0], [exchange(i) for i in range(len(CASES))], others)

    out = pl.pallas_call(
        finish,
        out_shape=jax.ShapeDtypeStruct((11, 32, 4096), BF16),
        in_specs=[smem, vmem, vmem],
        out_specs=hbm,
        scratch_shapes=[pltpu.VMEM((11, 32, 4096), BF16), pltpu.SemaphoreType.DMA((11,))],
        compiler_params=pltpu.CompilerParams(vmem_limit_bytes=40 << 20),
        cost_estimate=pl.CostEstimate(flops=1 << 30, bytes_accessed=6 << 20, transcendentals=0),
    )(choice, one, two)
    return out.transpose(1, 0, 2)


def solution(mesh):
    placed = (
        P("gx", "gy", "gz", None, None),
        P("gx", "gy", "gz", None),
        P("gx", "gy", "gz"),
        P(("gx", "gy", "gz"), None),
    )
    return jax.shard_map(
        local,
        mesh=mesh,
        in_specs=placed,
        out_specs=P(("gx", "gy", "gz"), None, None),
        check_vma=False,
    )
```

```python
import functools

import jax
import jax.numpy as jnp
from jax import lax
from jax.experimental import pallas as pl
from jax.experimental.pallas import tpu as pltpu
from jax.sharding import PartitionSpec as P

MESH = pl.DeviceIdType.MESH
F32 = jnp.float32
BF16 = jnp.bfloat16
GX, GY, GZ = 16, 4, 4
AXES = (
    ("gx", GX, lambda: lax.axis_index("gx")),
    ("gy", GY, lambda: lax.axis_index("gy")),
    ("gz", GZ, lambda: lax.axis_index("gz")),
)
GROUPS = GX // 2
CASES = (
    [tuple(range(GX))]
    + [(g, g + GROUPS) for g in range(0, GROUPS, 2)]
    + [(g, g + GROUPS, h, h + GROUPS) for g in range(GROUPS) for h in range(g + 1, GROUPS)]
)


def iota(shape, dim):
    return lax.broadcasted_iota(jnp.int32, shape, dim)


def ones_where(cond):
    return jnp.where(cond, 1.0, 0.0).astype(BF16)


def dot(a, b):
    return jnp.dot(a, b, preferred_element_type=F32)


def kernel(pair_hbm, route_hbm, a_hbm, p_hbm, recv, others, choice,
           pair_ref, route_ref, a_ref, p_ref, rows, anchors, nn, nr, ppt, hx, hy, hz, zs, gal, send, mine, seen_x, seen_y, seen_z,
           in_sem, hs_sem, hr_sem, s_sem, r_sem, fs_sem, fr_sem):
    gx, gy, gz = lax.axis_index("gx"), lax.axis_index("gy"), lax.axis_index("gz")

    load_p = pltpu.make_async_copy(p_hbm, p_ref, in_sem.at[0])
    load_a = pltpu.make_async_copy(a_hbm, a_ref, in_sem.at[1])
    load_route = pltpu.make_async_copy(route_hbm, route_ref, in_sem.at[2])
    load_pair = pltpu.make_async_copy(pair_hbm, pair_ref, in_sem.at[3])
    load_p.start()
    load_route.start()
    load_pair.start()
    load_a.start()
    barrier = pltpu.get_barrier_semaphore()
    for name, size, at in AXES:
        @pl.loop(1, size)
        def _(k):
            pl.semaphore_signal(barrier, inc=1, device_id={name: lax.rem(at() + k, size)}, device_id_type=MESH)
    sides = (
        (gx > 0, {"gx": gx - 1}), (gx < GX - 1, {"gx": gx + 1}),
        (gy > 0, {"gy": gy - 1}), (gy < GY - 1, {"gy": gy + 1}),
        (gz > 0, {"gz": gz - 1}), (gz < GZ - 1, {"gz": gz + 1}),
    )
    left = iota((64, 128), 1) < 64

    ci, ki = iota((64, 128), 0), iota((64, 128), 1)
    order = ones_where(((ki // 2) % 32 == ci // 2) & (ki // 64 == (ci + ki) % 2))
    ri, li = iota((128, 128), 0), iota((128, 128), 1)
    spread = ones_where(li % 64 == 2 * (ri % 32) + (ri // 32) % 2)
    same_z = li % 2 == ri // 64
    z_lane = (ri % 2) == (li // 64)
    half_row = (ri // 64) == (li // 64)

    load_p.wait()

    @pl.loop(0, 4)
    def _(x):
        tiles = []
        for y in range(4):
            raw = p_ref[4 * x + y].astype(F32)
            both = jnp.concatenate([raw, pltpu.roll(raw, 64, 1)], axis=0)
            tile = dot(order, jnp.where(z_lane, both, 0.0).astype(BF16))
            turned = pltpu.roll(tile, 64, 1)
            nn[x, y] = tile.astype(BF16)
            nr[4 * x + y] = turned.astype(BF16)
            tiles.append((tile, turned))
        for h in range(2):
            (low, high), (tile, turned) = tiles[2 * h], tiles[2 * h + 1]
            zs[0, 2 * x + h] = jnp.where(left, low, turned).astype(BF16)
            zs[1, 2 * x + h] = jnp.where(left, high, tile).astype(BF16)

    pl.semaphore_wait(barrier, GX + GY + GZ - 3)

    def tell(stage, k, seen):
        name, size, at = AXES[stage]
        return pltpu.make_async_remote_copy(
            src_ref=mine.at[stage], dst_ref=seen.at[k], send_sem=fs_sem.at[stage, k], recv_sem=fr_sem.at[stage, k],
            device_id={name: lax.rem(at() + k, size)}, device_id_type=MESH,
        )

    stages = (seen_x, seen_y, seen_z)

    def tell_all(stage):
        for k in range(1, AXES[stage][1]):
            tell(stage, k, stages[stage]).start()

    def hear_all(stage):
        flags = mine[stage]
        for k in range(1, AXES[stage][1]):
            tell(stage, k, stages[stage]).wait()
            flags = jnp.maximum(flags, stages[stage][k])
        return flags

    faces = (
        (nn.at[0], hx.at[1]), (nn.at[3], hx.at[0]),
        (nn.at[:, 0], hy.at[1]), (nn.at[:, 3], hy.at[0]),
        (zs.at[0], hz.at[1]), (zs.at[1], hz.at[0]),
    )
    own_halo = (hx.at[0], hx.at[1], hy.at[0], hy.at[1], hz.at[0], hz.at[1])

    def halo(i):
        source, target = faces[i]
        return pltpu.make_async_remote_copy(
            src_ref=source, dst_ref=target, send_sem=hs_sem.at[i], recv_sem=hr_sem.at[i],
            device_id=sides[i][1], device_id_type=MESH,
        )

    for i in (4, 5, 0, 1, 2, 3):
        @pl.when(sides[i][0])
        def _():
            halo(i).start()

        @pl.when(jnp.logical_not(sides[i][0]))
        def _():
            own_halo[i][...] = jnp.zeros(own_halo[i].shape, BF16)

    @pl.loop(0, 4)
    def _(x):
        for y in range(4):
            raw = p_ref[4 * x + y].astype(F32)
            twice = jnp.where(half_row, jnp.concatenate([raw, raw], axis=0), 0.0).astype(BF16)
            t = lax.dot_general(spread, twice, (((1,), (1,)), ((), ())), preferred_element_type=F32)
            ppt[4 * x + y] = jnp.where(same_z, t, 0.0).astype(BF16)

    lane = iota((8, 128), 1)

    def anchor(d, flags):
        def look(k, state):
            one, two = state
            hit = route_ref[k] == d
            two = jnp.where(hit & (one < 16) & (two == 16), k, two)
            one = jnp.where(hit & (one == 16), k, one)
            return one, two

        one, two = lax.fori_loop(0, 16, look, (jnp.int32(16), jnp.int32(16)), unroll=True)
        anchors[2 * d] = one
        anchors[2 * d + 1] = two
        return jnp.where((lane == d) & (two < 16), 1.0, flags)

    load_route.wait()
    mine[0] = lax.fori_loop(0, GX, anchor, jnp.zeros((8, 128), F32))
    tell_all(0)
    load_a.wait()
    load_pair.wait()
    zero = jnp.zeros((64, 128), BF16)
    left32 = iota((32, 128), 1) < 64

    def mix(xy, s, near_tile):
        wide = jnp.concatenate(
            [jnp.concatenate([near_tile, zero], axis=1), jnp.concatenate([zero, near_tile], axis=1)], axis=0
        )
        mixed = dot(a_ref[xy, s], wide).astype(BF16)
        return jnp.concatenate([mixed[:, :128], mixed[:, 128:]], axis=0)

    def keep(xy, s, g):
        gal[xy * 14 + 2 * s] = jnp.where(left32, g[0:32], pltpu.roll(g[32:64], 64, 1))
        gal[xy * 14 + 2 * s + 1] = jnp.where(left32, pltpu.roll(g[64:96], 64, 1), g[96:128])

    def product(xy, s, near_tile):
        keep(xy, s, dot(ppt[xy], mix(xy, s, near_tile)))

    def products(xy, s, t, near_s, near_t):
        g = dot(ppt[xy], jnp.concatenate([mix(xy, s, near_s), mix(xy, t, near_t)], axis=1))
        keep(xy, s, g[:, :128])
        keep(xy, t, g[:, 128:])

    @pl.loop(0, 2)
    def _(h):
        for u in range(2):
            for y in range(4):
                product(8 * h + 4 * u + y, 0, nn[2 * h + u, y])

    @pl.loop(0, 3)
    def _(i):
        for k in range(4):
            product(i * 4 + 4 + k, 1, nn[i, k])
            product(i * 4 + k, 2, nn[i + 1, k])

    def arrived(i):
        @pl.when(sides[i][0])
        def _():
            j = i ^ 1
            source, target = faces[j]
            pltpu.make_async_remote_copy(
                src_ref=source, dst_ref=target, send_sem=hs_sem.at[j], recv_sem=hr_sem.at[j],
                device_id=sides[i][1], device_id_type=MESH,
            ).wait_recv()

    arrived(4)
    arrived(5)

    @pl.loop(0, 4)
    def _(x):
        for q in range(2):
            below, above = hz[0, 2 * x + q].astype(F32), hz[1, 2 * x + q].astype(F32)
            below = (below, pltpu.roll(below, 64, 1))
            above = (pltpu.roll(above, 64, 1), above)
            for u in range(2):
                xy = 4 * x + 2 * q + u
                own = nr[xy]
                products(xy, 5, 6, jnp.where(left, below[u].astype(BF16), own), jnp.where(left, own, above[u].astype(BF16)))

    def place_of(k):
        a, b, z, t = k // 8, (k // 4) % 2, (k // 2) % 2, k % 2
        along = pair_ref[a, b, z] == 0
        corner = a * 8 + b * 2
        first = jnp.where(along, corner + t, corner + 4 * t)
        second = jnp.where(along, corner + 4 + t, corner + 4 * t + 1)
        return along, first, second, lambda xy, s: gal[xy * 14 + 2 * s + z]

    @pl.loop(0, 16)
    def _(k):
        along, first, second, block = place_of(k)
        for i, xy in enumerate((first, second)):
            for j in range(2):
                rows[k, 2 * i + j] = block(xy, 5 + j).astype(BF16)

    parts = (pl.ds(0, 4), pl.ds(4, 7))

    def outgoing(part, k):
        return pltpu.make_async_remote_copy(
            src_ref=send.at[k, parts[part]], dst_ref=recv.at[gx, parts[part]],
            send_sem=s_sem.at[part, k], recv_sem=r_sem.at[part, k],
            device_id={"gx": lax.rem(gx + k, GX)}, device_id_type=MESH,
        )

    def post(part):
        @pl.loop(1, GX)
        def _(k):
            send[k, parts[part]] = pick(rows, anchors, lax.rem(gx + k, GX), 0, parts[part])
            outgoing(part, k).start()

    post(0)

    @pl.loop(0, 3)
    def _(i):
        for k in range(4):
            product(k * 4 + i + 1, 3, nn[k, i])
            product(k * 4 + i, 4, nn[k, i + 1])

    mine[1] = hear_all(0)
    tell_all(1)
    for i in range(4):
        arrived(i)

    @pl.loop(0, 4)
    def _(k):
        product(k, 1, hx[0, k])
        product(12 + k, 2, hx[1, k])
        product(k * 4, 3, hy[0, k])
        product(k * 4 + 3, 4, hy[1, k])

    mine[2] = hear_all(1)
    tell_all(2)

    @pl.loop(0, 16)
    def _(k):
        along, first, second, block = place_of(k)
        rows[k, 4] = (
            block(first, 0) + block(second, 0)
            + block(first, jnp.where(along, 2, 4)) + block(second, jnp.where(along, 1, 3))
        ).astype(BF16)
        slots_x = ((1, 3, 4), (2, 3, 4))
        slots_y = ((1, 2, 3), (1, 2, 4))
        for i, xy in enumerate((first, second)):
            for j in range(3):
                rows[k, 5 + 3 * i + j] = block(xy, jnp.where(along, slots_x[i][j], slots_y[i][j])).astype(BF16)

    post(1)
    recv[gx] = pick(rows, anchors, gx, 0)

    @pl.loop(0, GX)
    def _(d):
        others[d] = pick(rows, anchors, d, 1)

    flags = hear_all(2)[0:1]
    flags = jnp.maximum(flags, pltpu.roll(flags, 128 - GROUPS, 1))
    flags = jnp.where(iota((1, 128), 1) < GROUPS, flags, 0.0)
    place = iota((1, 128), 1).astype(F32)
    count = jnp.sum(flags)
    high = jnp.max(jnp.where(flags > 0, place, 0.0))
    low = jnp.where(count > 0.5, jnp.min(jnp.where(flags > 0, place, 128.0)), 0.0)
    alone, half = count < 1.5, GROUPS // 2
    odd = low - 2.0 * jnp.floor(low * 0.5) > 0.5
    even_case = 1.0 + low * 0.5
    low = jnp.where(alone & (low >= half), low - half, low)
    high = jnp.where(alone, low + half, high)
    two = 1.0 + half + low * (2 * GROUPS - 1 - low) * 0.5 + (high - low - 1.0)
    case = jnp.where(count > 2.5, 0.0, jnp.where(alone & jnp.logical_not(odd), even_case, two))
    choice[0] = case.astype(jnp.int32)
    choice[1] = (jnp.sum(jnp.where(place == lax.rem(gx, GROUPS).astype(F32), flags, 0.0)) > 0.5).astype(jnp.int32)

    for i in range(6):
        @pl.when(sides[i][0])
        def _():
            halo(i).wait_send()

    @pl.loop(1, GX)
    def _(k):
        outgoing(0, k).wait()
        outgoing(1, k).wait()


def pick(rows, anchors, d, c, part=slice(None)):
    k = anchors[2 * d + c]
    row = rows[jnp.minimum(k, 15), part]
    return jnp.where(k < 16, row, jnp.zeros_like(row))


def second(dests, rows, recv, s_sem, r_sem, own_sem):
    gx = lax.axis_index("gx")
    barrier = pltpu.get_barrier_semaphore()
    number = len(dests)
    hot = functools.reduce(jnp.logical_or, [gx == d for d in dests]) if number < GX else gx >= 0

    @pl.when(hot)
    def _():
        @pl.loop(1, GX)
        def _(k):
            pl.semaphore_signal(barrier, inc=1, device_id={"gx": lax.rem(gx + k, GX)}, device_id_type=MESH)

    def copy(source, target, device):
        return pltpu.make_async_remote_copy(
            src_ref=source, dst_ref=target, send_sem=s_sem, recv_sem=r_sem,
            device_id={"gx": device}, device_id_type=MESH,
        )

    def bytes_of(n):
        return copy(rows.at[pl.ds(0, n)], recv.at[pl.ds(0, n)], 0)

    pl.semaphore_wait(barrier, number - hot.astype(jnp.int32))

    @pl.loop(0, number)
    def _(i):
        if number == GX:
            d = lax.rem(gx + i, GX)
        else:
            d = dests[0] + GROUPS * lax.rem(i, 2)
            d = jnp.where(i < 2, d, d + dests[-2] - dests[0])

        @pl.when(gx != d)
        def _():
            copy(rows.at[d], recv.at[gx], d).start()

    @pl.when(hot)
    def _():
        own = pltpu.make_async_copy(rows.at[gx], recv.at[gx], own_sem)
        own.start()
        own.wait()
        bytes_of(GX - 1).wait_recv()
        bytes_of(number - 1).wait_send()

    @pl.when(jnp.logical_not(hot))
    def _():
        bytes_of(number).wait_send()


def finish(choice, one, two, out_hbm, out, sem):
    pi, qi = iota((256, 256), 0), iota((256, 256), 1)
    turn = ones_where((qi % 32 == pi // 8) & (qi // 32 == pi % 8))
    zero = jnp.zeros((32, 128), BF16)

    def store(b):
        return pltpu.make_async_copy(out.at[b], out_hbm.at[b], sem.at[b])

    def turned(hot):
        @pl.loop(0, 11)
        def _(i):
            b = jnp.where(i < 4, 4 + i % 2 + 5 * (i // 2), jnp.where(i < 8, i - 4, i - 2))
            for g in range(2):
                x = [
                    jnp.concatenate(
                        [t for s in range(4) for t in (one[8 * g + 4 * h + s, i], two[8 * g + 4 * h + s, i] if hot else zero)],
                        axis=0,
                    )
                    for h in range(2)
                ]
                y = dot(turn, jnp.concatenate(x, axis=1))
                tile = jnp.concatenate([y[:, :128].reshape(32, 8, 128), y[:, 128:].reshape(32, 8, 128)], axis=1).astype(BF16)
                for j in range(32):
                    out[b, pl.ds(16 * g, 16), pl.ds(128 * j, 128)] = tile[j]
            store(b).start()

    pl.when(choice[1] == 1)(lambda: turned(True))
    pl.when(choice[1] != 1)(lambda: turned(False))

    @pl.loop(0, 11)
    def _(b):
        store(b).wait()


def local(a_blocks, prolong, pairing, route):
    a = a_blocks.reshape(4, 4, 2, 7, 32, 128).transpose(0, 1, 3, 4, 2, 5).reshape(16, 7, 64, 128)
    p = prolong.reshape(4, 4, 2, 32, 128).transpose(0, 1, 3, 2, 4).reshape(16, 64, 128)
    smem = pl.BlockSpec(memory_space=pltpu.SMEM)
    vmem = pl.BlockSpec(memory_space=pltpu.VMEM)
    hbm = pl.BlockSpec(memory_space=pltpu.HBM)
    row_set = jax.ShapeDtypeStruct((16, 11, 32, 128), BF16)
    one, others, choice = pl.pallas_call(
        kernel,
        out_shape=(row_set, row_set, jax.ShapeDtypeStruct((2,), jnp.int32)),
        in_specs=[hbm, hbm, hbm, hbm],
        out_specs=(vmem, vmem, smem),
        scratch_shapes=[
            pltpu.SMEM((2, 2, 2), jnp.int32),
            pltpu.SMEM((16,), jnp.int32),
            pltpu.VMEM((16, 7, 64, 128), BF16),
            pltpu.VMEM((16, 64, 128), BF16),
            pltpu.VMEM((16, 11, 32, 128), BF16),
            pltpu.SMEM((32,), jnp.int32),
            pltpu.VMEM((4, 4, 64, 128), BF16),
            pltpu.VMEM((16, 64, 128), BF16),
            pltpu.VMEM((16, 128, 128), BF16),
            pltpu.VMEM((2, 4, 64, 128), BF16),
            pltpu.VMEM((2, 4, 64, 128), BF16),
            pltpu.VMEM((2, 8, 64, 128), BF16),
            pltpu.VMEM((2, 8, 64, 128), BF16),
            pltpu.VMEM((224, 32, 128), F32),
            pltpu.VMEM((16, 11, 32, 128), BF16),
            pltpu.VMEM((3, 8, 128), F32),
            pltpu.VMEM((GX, 8, 128), F32),
            pltpu.VMEM((GY, 8, 128), F32),
            pltpu.VMEM((GZ, 8, 128), F32),
            pltpu.SemaphoreType.DMA((4,)),
            pltpu.SemaphoreType.DMA((6,)),
            pltpu.SemaphoreType.DMA((6,)),
            pltpu.SemaphoreType.DMA((2, 16)),
            pltpu.SemaphoreType.DMA((2, 16)),
            pltpu.SemaphoreType.DMA((3, 16)),
            pltpu.SemaphoreType.DMA((3, 16)),
        ],
        compiler_params=pltpu.CompilerParams(
            collective_id=0, has_side_effects=True, vmem_limit_bytes=60 << 20
        ),
        cost_estimate=pl.CostEstimate(flops=1 << 30, bytes_accessed=8 << 20, transcendentals=0),
    )(pairing, route.reshape(16), a, p)

    def exchange(number):
        dests = CASES[number]
        return pl.pallas_call(
            functools.partial(second, dests),
            out_shape=row_set,
            in_specs=[vmem],
            out_specs=vmem,
            scratch_shapes=[
                pltpu.SemaphoreType.DMA,
                pltpu.SemaphoreType.DMA,
                pltpu.SemaphoreType.DMA,
            ],
            compiler_params=pltpu.CompilerParams(
                collective_id=1 + number, has_side_effects=True, vmem_limit_bytes=40 << 20
            ),
            cost_estimate=pl.CostEstimate(flops=0, bytes_accessed=4 << 20, transcendentals=0),
        )

    two = lax.switch(choice[0], [exchange(i) for i in range(len(CASES))], others)

    out = pl.pallas_call(
        finish,
        out_shape=jax.ShapeDtypeStruct((11, 32, 4096), BF16),
        in_specs=[smem, vmem, vmem],
        out_specs=hbm,
        scratch_shapes=[pltpu.VMEM((11, 32, 4096), BF16), pltpu.SemaphoreType.DMA((11,))],
        compiler_params=pltpu.CompilerParams(vmem_limit_bytes=40 << 20),
        cost_estimate=pl.CostEstimate(flops=1 << 30, bytes_accessed=6 << 20, transcendentals=0),
    )(choice, one, two)
    return out.transpose(1, 0, 2)


def solution(mesh):
    placed = (
        P("gx", "gy", "gz", None, None),
        P("gx", "gy", "gz", None),
        P("gx", "gy", "gz"),
        P(("gx", "gy", "gz"), None),
    )
    return jax.shard_map(
        local,
        mesh=mesh,
        in_specs=placed,
        out_specs=P(("gx", "gy", "gz"), None, None),
        check_vma=False,
    )
```

```python
import functools

import jax
import jax.numpy as jnp
from jax import lax
from jax.experimental import pallas as pl
from jax.experimental.pallas import tpu as pltpu
from jax.sharding import PartitionSpec as P

MESH = pl.DeviceIdType.MESH
F32 = jnp.float32
BF16 = jnp.bfloat16
GX, GY, GZ = 16, 4, 4
AXES = (
    ("gx", GX, lambda: lax.axis_index("gx")),
    ("gy", GY, lambda: lax.axis_index("gy")),
    ("gz", GZ, lambda: lax.axis_index("gz")),
)
GROUPS = GX // 2
CASES = (
    [tuple(range(GX))]
    + [(g, g + GROUPS) for g in range(0, GROUPS, 2)]
    + [(g, g + GROUPS, h, h + GROUPS) for g in range(GROUPS) for h in range(g + 1, GROUPS)]
)


def iota(shape, dim):
    return lax.broadcasted_iota(jnp.int32, shape, dim)


def ones_where(cond):
    return jnp.where(cond, 1.0, 0.0).astype(BF16)


def dot(a, b):
    return jnp.dot(a, b, preferred_element_type=F32)


def kernel(pair_hbm, route_hbm, a_hbm, p_hbm, recv, others, choice,
           pair_ref, route_ref, a_ref, p_ref, rows, anchors, nn, nr, ppt, hx, hy, hz, zs, gal, send, mine, seen_x, seen_y, seen_z,
           in_sem, hs_sem, hr_sem, s_sem, r_sem, fs_sem, fr_sem):
    gx, gy, gz = lax.axis_index("gx"), lax.axis_index("gy"), lax.axis_index("gz")

    load_p = pltpu.make_async_copy(p_hbm, p_ref, in_sem.at[0])
    load_a = pltpu.make_async_copy(a_hbm, a_ref, in_sem.at[1])
    load_route = pltpu.make_async_copy(route_hbm, route_ref, in_sem.at[2])
    load_pair = pltpu.make_async_copy(pair_hbm, pair_ref, in_sem.at[3])
    load_p.start()
    load_route.start()
    load_pair.start()
    load_a.start()
    barrier = pltpu.get_barrier_semaphore()
    for name, size, at in AXES:
        @pl.loop(1, size)
        def _(k):
            pl.semaphore_signal(barrier, inc=1, device_id={name: lax.rem(at() + k, size)}, device_id_type=MESH)
    sides = (
        (gx > 0, {"gx": gx - 1}), (gx < GX - 1, {"gx": gx + 1}),
        (gy > 0, {"gy": gy - 1}), (gy < GY - 1, {"gy": gy + 1}),
        (gz > 0, {"gz": gz - 1}), (gz < GZ - 1, {"gz": gz + 1}),
    )
    left = iota((64, 128), 1) < 64

    ci, ki = iota((64, 128), 0), iota((64, 128), 1)
    order = ones_where(((ki // 2) % 32 == ci // 2) & (ki // 64 == (ci + ki) % 2))
    ri, li = iota((128, 128), 0), iota((128, 128), 1)
    spread = ones_where(li % 64 == 2 * (ri % 32) + (ri // 32) % 2)
    same_z = li % 2 == ri // 64
    z_lane = (ri % 2) == (li // 64)
    half_row = (ri // 64) == (li // 64)

    load_p.wait()

    @pl.loop(0, 4)
    def _(x):
        tiles = []
        for y in range(4):
            raw = p_ref[4 * x + y].astype(F32)
            both = jnp.concatenate([raw, pltpu.roll(raw, 64, 1)], axis=0)
            tile = dot(order, jnp.where(z_lane, both, 0.0).astype(BF16))
            turned = pltpu.roll(tile, 64, 1)
            nn[x, y] = tile.astype(BF16)
            nr[4 * x + y] = turned.astype(BF16)
            tiles.append((tile, turned))
        for h in range(2):
            (low, high), (tile, turned) = tiles[2 * h], tiles[2 * h + 1]
            zs[0, 2 * x + h] = jnp.where(left, low, turned).astype(BF16)
            zs[1, 2 * x + h] = jnp.where(left, high, tile).astype(BF16)

    pl.semaphore_wait(barrier, GX + GY + GZ - 3)

    def tell(stage, k, seen):
        name, size, at = AXES[stage]
        return pltpu.make_async_remote_copy(
            src_ref=mine.at[stage], dst_ref=seen.at[k], send_sem=fs_sem.at[stage, k], recv_sem=fr_sem.at[stage, k],
            device_id={name: lax.rem(at() + k, size)}, device_id_type=MESH,
        )

    stages = (seen_x, seen_y, seen_z)

    def tell_all(stage):
        for k in range(1, AXES[stage][1]):
            tell(stage, k, stages[stage]).start()

    def hear_all(stage):
        flags = mine[stage]
        for k in range(1, AXES[stage][1]):
            tell(stage, k, stages[stage]).wait()
            flags = jnp.maximum(flags, stages[stage][k])
        return flags

    faces = (
        (nn.at[0], hx.at[1]), (nn.at[3], hx.at[0]),
        (nn.at[:, 0], hy.at[1]), (nn.at[:, 3], hy.at[0]),
        (zs.at[0], hz.at[1]), (zs.at[1], hz.at[0]),
    )
    own_halo = (hx.at[0], hx.at[1], hy.at[0], hy.at[1], hz.at[0], hz.at[1])

    def halo(i):
        source, target = faces[i]
        return pltpu.make_async_remote_copy(
            src_ref=source, dst_ref=target, send_sem=hs_sem.at[i], recv_sem=hr_sem.at[i],
            device_id=sides[i][1], device_id_type=MESH,
        )

    for i in (4, 5, 0, 1, 2, 3):
        @pl.when(sides[i][0])
        def _():
            halo(i).start()

        @pl.when(jnp.logical_not(sides[i][0]))
        def _():
            own_halo[i][...] = jnp.zeros(own_halo[i].shape, BF16)

    @pl.loop(0, 4)
    def _(x):
        for y in range(4):
            raw = p_ref[4 * x + y].astype(F32)
            twice = jnp.where(half_row, jnp.concatenate([raw, raw], axis=0), 0.0).astype(BF16)
            t = lax.dot_general(spread, twice, (((1,), (1,)), ((), ())), preferred_element_type=F32)
            ppt[4 * x + y] = jnp.where(same_z, t, 0.0).astype(BF16)

    lane = iota((8, 128), 1)

    def anchor(d, flags):
        def look(k, state):
            one, two = state
            hit = route_ref[k] == d
            two = jnp.where(hit & (one < 16) & (two == 16), k, two)
            one = jnp.where(hit & (one == 16), k, one)
            return one, two

        one, two = lax.fori_loop(0, 16, look, (jnp.int32(16), jnp.int32(16)), unroll=True)
        anchors[2 * d] = one
        anchors[2 * d + 1] = two
        return jnp.where((lane == d) & (two < 16), 1.0, flags)

    load_route.wait()
    mine[0] = lax.fori_loop(0, GX, anchor, jnp.zeros((8, 128), F32))
    tell_all(0)
    load_a.wait()
    load_pair.wait()
    zero = jnp.zeros((64, 128), BF16)
    left32 = iota((32, 128), 1) < 64

    def mix(xy, s, near_tile):
        wide = jnp.concatenate(
            [jnp.concatenate([near_tile, zero], axis=1), jnp.concatenate([zero, near_tile], axis=1)], axis=0
        )
        mixed = dot(a_ref[xy, s], wide).astype(BF16)
        return jnp.concatenate([mixed[:, :128], mixed[:, 128:]], axis=0)

    def keep(xy, s, g):
        gal[xy * 14 + 2 * s] = jnp.where(left32, g[0:32], pltpu.roll(g[32:64], 64, 1))
        gal[xy * 14 + 2 * s + 1] = jnp.where(left32, pltpu.roll(g[64:96], 64, 1), g[96:128])

    def product(xy, s, near_tile):
        keep(xy, s, dot(ppt[xy], mix(xy, s, near_tile)))

    def products(xy, s, t, near_s, near_t):
        g = dot(ppt[xy], jnp.concatenate([mix(xy, s, near_s), mix(xy, t, near_t)], axis=1))
        keep(xy, s, g[:, :128])
        keep(xy, t, g[:, 128:])

    @pl.loop(0, 2)
    def _(h):
        for u in range(2):
            for y in range(4):
                product(8 * h + 4 * u + y, 0, nn[2 * h + u, y])

    @pl.loop(0, 3)
    def _(i):
        for k in range(4):
            product(i * 4 + 4 + k, 1, nn[i, k])
            product(i * 4 + k, 2, nn[i + 1, k])

    def arrived(i):
        @pl.when(sides[i][0])
        def _():
            j = i ^ 1
            source, target = faces[j]
            pltpu.make_async_remote_copy(
                src_ref=source, dst_ref=target, send_sem=hs_sem.at[j], recv_sem=hr_sem.at[j],
                device_id=sides[i][1], device_id_type=MESH,
            ).wait_recv()

    arrived(4)
    arrived(5)

    @pl.loop(0, 4)
    def _(x):
        for q in range(2):
            below, above = hz[0, 2 * x + q].astype(F32), hz[1, 2 * x + q].astype(F32)
            below = (below, pltpu.roll(below, 64, 1))
            above = (pltpu.roll(above, 64, 1), above)
            for u in range(2):
                xy = 4 * x + 2 * q + u
                own = nr[xy]
                products(xy, 5, 6, jnp.where(left, below[u].astype(BF16), own), jnp.where(left, own, above[u].astype(BF16)))

    def place_of(k):
        a, b, z, t = k // 8, (k // 4) % 2, (k // 2) % 2, k % 2
        along = pair_ref[a, b, z] == 0
        corner = a * 8 + b * 2
        first = jnp.where(along, corner + t, corner + 4 * t)
        second = jnp.where(along, corner + 4 + t, corner + 4 * t + 1)
        return along, first, second, lambda xy, s: gal[xy * 14 + 2 * s + z]

    @pl.loop(0, 16)
    def _(k):
        along, first, second, block = place_of(k)
        for i, xy in enumerate((first, second)):
            for j in range(2):
                rows[k, 2 * i + j] = block(xy, 5 + j).astype(BF16)

    parts = (pl.ds(0, 4), pl.ds(4, 7))

    def outgoing(part, k):
        return pltpu.make_async_remote_copy(
            src_ref=send.at[k, parts[part]], dst_ref=recv.at[gx, parts[part]],
            send_sem=s_sem.at[part, k], recv_sem=r_sem.at[part, k],
            device_id={"gx": lax.rem(gx + k, GX)}, device_id_type=MESH,
        )

    def post(part):
        @pl.loop(1, GX)
        def _(k):
            send[k, parts[part]] = pick(rows, anchors, lax.rem(gx + k, GX), 0, parts[part])
            outgoing(part, k).start()

    post(0)

    @pl.loop(0, 3)
    def _(i):
        for k in range(4):
            product(k * 4 + i + 1, 3, nn[k, i])
            product(k * 4 + i, 4, nn[k, i + 1])

    mine[1] = hear_all(0)
    tell_all(1)
    for i in range(4):
        arrived(i)

    @pl.loop(0, 4)
    def _(k):
        product(k, 1, hx[0, k])
        product(12 + k, 2, hx[1, k])
        product(k * 4, 3, hy[0, k])
        product(k * 4 + 3, 4, hy[1, k])

    mine[2] = hear_all(1)
    tell_all(2)

    @pl.loop(0, 16)
    def _(k):
        along, first, second, block = place_of(k)
        rows[k, 4] = (
            block(first, 0) + block(second, 0)
            + block(first, jnp.where(along, 2, 4)) + block(second, jnp.where(along, 1, 3))
        ).astype(BF16)
        slots_x = ((1, 3, 4), (2, 3, 4))
        slots_y = ((1, 2, 3), (1, 2, 4))
        for i, xy in enumerate((first, second)):
            for j in range(3):
                rows[k, 5 + 3 * i + j] = block(xy, jnp.where(along, slots_x[i][j], slots_y[i][j])).astype(BF16)

    post(1)
    recv[gx] = pick(rows, anchors, gx, 0)

    @pl.loop(0, GX)
    def _(d):
        others[d] = pick(rows, anchors, d, 1)

    flags = hear_all(2)[0:1]
    flags = jnp.maximum(flags, pltpu.roll(flags, 128 - GROUPS, 1))
    flags = jnp.where(iota((1, 128), 1) < GROUPS, flags, 0.0)
    place = iota((1, 128), 1).astype(F32)
    count = jnp.sum(flags)
    high = jnp.max(jnp.where(flags > 0, place, 0.0))
    low = jnp.where(count > 0.5, jnp.min(jnp.where(flags > 0, place, 128.0)), 0.0)
    alone, half = count < 1.5, GROUPS // 2
    odd = low - 2.0 * jnp.floor(low * 0.5) > 0.5
    even_case = 1.0 + low * 0.5
    low = jnp.where(alone & (low >= half), low - half, low)
    high = jnp.where(alone, low + half, high)
    two = 1.0 + half + low * (2 * GROUPS - 1 - low) * 0.5 + (high - low - 1.0)
    case = jnp.where(count > 2.5, 0.0, jnp.where(alone & jnp.logical_not(odd), even_case, two))
    choice[0] = case.astype(jnp.int32)
    choice[1] = (jnp.sum(jnp.where(place == lax.rem(gx, GROUPS).astype(F32), flags, 0.0)) > 0.5).astype(jnp.int32)

    for i in range(6):
        @pl.when(sides[i][0])
        def _():
            halo(i).wait_send()

    @pl.loop(1, GX)
    def _(k):
        outgoing(0, k).wait()
        outgoing(1, k).wait()


def pick(rows, anchors, d, c, part=slice(None)):
    k = anchors[2 * d + c]
    row = rows[jnp.minimum(k, 15), part]
    return jnp.where(k < 16, row, jnp.zeros_like(row))


def second(dests, rows, recv, s_sem, r_sem, own_sem):
    gx = lax.axis_index("gx")
    barrier = pltpu.get_barrier_semaphore()
    number = len(dests)
    hot = functools.reduce(jnp.logical_or, [gx == d for d in dests]) if number < GX else gx >= 0

    @pl.when(hot)
    def _():
        @pl.loop(1, GX)
        def _(k):
            pl.semaphore_signal(barrier, inc=1, device_id={"gx": lax.rem(gx + k, GX)}, device_id_type=MESH)

    def copy(source, target, device):
        return pltpu.make_async_remote_copy(
            src_ref=source, dst_ref=target, send_sem=s_sem, recv_sem=r_sem,
            device_id={"gx": device}, device_id_type=MESH,
        )

    def bytes_of(n):
        return copy(rows.at[pl.ds(0, n)], recv.at[pl.ds(0, n)], 0)

    away = lax.rem(gx // 2 - dests[0] // 2 + GROUPS, GROUPS)
    tie = (away == 2) | (away == 6)
    far = (((away > 2) & (away < 6)) | (tie & (gx % 2 == 1))).astype(jnp.int32)
    pl.semaphore_wait(barrier, number - hot.astype(jnp.int32))

    @pl.loop(0, number)
    def _(i):
        if number == GX:
            d = lax.rem(gx + i, GX)
        else:
            d = dests[0] + GROUPS * lax.rem(i + far, 2)
            d = jnp.where(i < 2, d, d + dests[-2] - dests[0])

        @pl.when(gx != d)
        def _():
            copy(rows.at[d], recv.at[gx], d).start()

    @pl.when(hot)
    def _():
        own = pltpu.make_async_copy(rows.at[gx], recv.at[gx], own_sem)
        own.start()
        bytes_of(GX - 1).wait_recv()
        own.wait()
        bytes_of(number - 1).wait_send()

    @pl.when(jnp.logical_not(hot))
    def _():
        bytes_of(number).wait_send()


def finish(choice, one, two, out_hbm, out, sem):
    pi, qi = iota((256, 256), 0), iota((256, 256), 1)
    turn = ones_where((qi % 32 == pi // 8) & (qi // 32 == pi % 8))
    zero = jnp.zeros((32, 128), BF16)

    def store(b):
        return pltpu.make_async_copy(out.at[b], out_hbm.at[b], sem.at[b])

    def turned(hot):
        @pl.loop(0, 11)
        def _(i):
            b = jnp.where(i < 4, 4 + i % 2 + 5 * (i // 2), jnp.where(i < 8, i - 4, i - 2))
            for g in range(2):
                x = [
                    jnp.concatenate(
                        [t for s in range(4) for t in (one[8 * g + 4 * h + s, i], two[8 * g + 4 * h + s, i] if hot else zero)],
                        axis=0,
                    )
                    for h in range(2)
                ]
                y = dot(turn, jnp.concatenate(x, axis=1))
                tile = jnp.concatenate([y[:, :128].reshape(32, 8, 128), y[:, 128:].reshape(32, 8, 128)], axis=1).astype(BF16)
                for j in range(32):
                    out[b, pl.ds(16 * g, 16), pl.ds(128 * j, 128)] = tile[j]
            store(b).start()

    pl.when(choice[1] == 1)(lambda: turned(True))
    pl.when(choice[1] != 1)(lambda: turned(False))

    @pl.loop(0, 11)
    def _(b):
        store(b).wait()


def local(a_blocks, prolong, pairing, route):
    a = a_blocks.reshape(4, 4, 2, 7, 32, 128).transpose(0, 1, 3, 4, 2, 5).reshape(16, 7, 64, 128)
    p = prolong.reshape(4, 4, 2, 32, 128).transpose(0, 1, 3, 2, 4).reshape(16, 64, 128)
    smem = pl.BlockSpec(memory_space=pltpu.SMEM)
    vmem = pl.BlockSpec(memory_space=pltpu.VMEM)
    hbm = pl.BlockSpec(memory_space=pltpu.HBM)
    row_set = jax.ShapeDtypeStruct((16, 11, 32, 128), BF16)
    one, others, choice = pl.pallas_call(
        kernel,
        out_shape=(row_set, row_set, jax.ShapeDtypeStruct((2,), jnp.int32)),
        in_specs=[hbm, hbm, hbm, hbm],
        out_specs=(vmem, vmem, smem),
        scratch_shapes=[
            pltpu.SMEM((2, 2, 2), jnp.int32),
            pltpu.SMEM((16,), jnp.int32),
            pltpu.VMEM((16, 7, 64, 128), BF16),
            pltpu.VMEM((16, 64, 128), BF16),
            pltpu.VMEM((16, 11, 32, 128), BF16),
            pltpu.SMEM((32,), jnp.int32),
            pltpu.VMEM((4, 4, 64, 128), BF16),
            pltpu.VMEM((16, 64, 128), BF16),
            pltpu.VMEM((16, 128, 128), BF16),
            pltpu.VMEM((2, 4, 64, 128), BF16),
            pltpu.VMEM((2, 4, 64, 128), BF16),
            pltpu.VMEM((2, 8, 64, 128), BF16),
            pltpu.VMEM((2, 8, 64, 128), BF16),
            pltpu.VMEM((224, 32, 128), F32),
            pltpu.VMEM((16, 11, 32, 128), BF16),
            pltpu.VMEM((3, 8, 128), F32),
            pltpu.VMEM((GX, 8, 128), F32),
            pltpu.VMEM((GY, 8, 128), F32),
            pltpu.VMEM((GZ, 8, 128), F32),
            pltpu.SemaphoreType.DMA((4,)),
            pltpu.SemaphoreType.DMA((6,)),
            pltpu.SemaphoreType.DMA((6,)),
            pltpu.SemaphoreType.DMA((2, 16)),
            pltpu.SemaphoreType.DMA((2, 16)),
            pltpu.SemaphoreType.DMA((3, 16)),
            pltpu.SemaphoreType.DMA((3, 16)),
        ],
        compiler_params=pltpu.CompilerParams(
            collective_id=0, has_side_effects=True, vmem_limit_bytes=60 << 20
        ),
        cost_estimate=pl.CostEstimate(flops=1 << 30, bytes_accessed=8 << 20, transcendentals=0),
    )(pairing, route.reshape(16), a, p)

    def exchange(number):
        dests = CASES[number]
        return pl.pallas_call(
            functools.partial(second, dests),
            out_shape=row_set,
            in_specs=[vmem],
            out_specs=vmem,
            scratch_shapes=[
                pltpu.SemaphoreType.DMA,
                pltpu.SemaphoreType.DMA,
                pltpu.SemaphoreType.DMA,
            ],
            compiler_params=pltpu.CompilerParams(
                collective_id=1 + number, has_side_effects=True, vmem_limit_bytes=40 << 20
            ),
            cost_estimate=pl.CostEstimate(flops=0, bytes_accessed=4 << 20, transcendentals=0),
        )

    two = lax.switch(choice[0], [exchange(i) for i in range(len(CASES))], others)

    out = pl.pallas_call(
        finish,
        out_shape=jax.ShapeDtypeStruct((11, 32, 4096), BF16),
        in_specs=[smem, vmem, vmem],
        out_specs=hbm,
        scratch_shapes=[pltpu.VMEM((11, 32, 4096), BF16), pltpu.SemaphoreType.DMA((11,))],
        compiler_params=pltpu.CompilerParams(vmem_limit_bytes=40 << 20),
        cost_estimate=pl.CostEstimate(flops=1 << 30, bytes_accessed=6 << 20, transcendentals=0),
    )(choice, one, two)
    return out.transpose(1, 0, 2)


def solution(mesh):
    placed = (
        P("gx", "gy", "gz", None, None),
        P("gx", "gy", "gz", None),
        P("gx", "gy", "gz"),
        P(("gx", "gy", "gz"), None),
    )
    return jax.shard_map(
        local,
        mesh=mesh,
        in_specs=placed,
        out_specs=P(("gx", "gy", "gz"), None, None),
        check_vma=False,
    )
```
